128 devices in a mesh: rep: 8 (over z, y_lo), shard: 16 (over y_hi, x, core).
Axes of the slice: x: 4, y: 4 (y_hi: 2, y_lo: 2; y = y_hi * 2 + y_lo), z: 4, core: 2. Of those that a mesh axis runs over, the one named last changes fastest.
Arguments:
- tokens: bfloat16 [8, 2048, 1600], P('rep', 'shard'), may hold values from -6 to 6
- segments: int32 [8, 2048], P('rep', 'shard'), may hold values from 0 to 31, as said below
- input_gain: bfloat16 [1600], P('shard'), may hold values from 0.5 to 1.5
- attention_weight: bfloat16 [1600, 2240], P('shard'), may hold values from -0.15625 to 0.15625
- attend_out: bfloat16 [1600, 1600], P('shard'), may hold values from -0.15625 to 0.15625
- mixer_weight: bfloat16 [1600, 6400], P('shard'), may hold values from -0.15625 to 0.15625
- param_weight: bfloat16 [1600, 82], P('shard'), may hold values from -0.15625 to 0.15625
- mixer_out: bfloat16 [3200, 1600], P('shard'), may hold values from -0.109375 to 0.109375
- attend_gain: bfloat16 [1600], P('shard'), may hold values from 0.5 to 1.5
- mixer_gain: bfloat16 [1600], P('shard'), may hold values from 0.5 to 1.5
- feed_gain: bfloat16 [1600], P('shard'), may hold values from 0.5 to 1.5
- gateup_weight: bfloat16 [1600, 2, 5504], P(None, None, 'shard'), may hold values from -0.15625 to 0.15625
- down_weight: bfloat16 [5504, 1600], P('shard'), may hold values from -0.078125 to 0.078125
- decay_log: float32 [50], replicated, may hold values from -5.3 to -0.7
- step_bias: float32 [50], replicated, may hold values from -3 to -1
- skip_gain: float32 [50], replicated, may hold values from 0.5 to 1.5
- cotangent: bfloat16 [8, 2048, 1600], P('rep', 'shard'), may hold values from -6 to 6
Outputs:
- output: bfloat16 [8, 2048, 1600], P('rep', 'shard')
- grad_tokens: bfloat16 [8, 2048, 1600], P('rep', 'shard')
- grad_input_gain: float32 [1600], P('shard')
- grad_attend_weight: float32 [1600, 2240], P('shard')
- grad_attend_out: float32 [1600, 1600], P('shard')
- grad_mixer_weight: float32 [1600, 6400], P('shard')
- grad_param_weight: float32 [1600, 82], P('shard')
- grad_mixer_out: float32 [3200, 1600], P('shard')
- grad_attend_gain: float32 [1600], P('shard')
- grad_mixer_gain: float32 [1600], P('shard')
- grad_feed_gain: float32 [1600], P('shard')
- grad_gateup_weight: float32 [1600, 2, 5504], P(None, None, 'shard')
- grad_down_weight: float32 [5504, 1600], P('shard')
- grad_decay_log: float32 [50], replicated
- grad_step_bias: float32 [50], replicated
- grad_skip_gain: float32 [50], replicated
The draws below stay inside these ranges and needn't reach their ends.
Inputs may be any that keep to these rules, and one draw needn't show every extreme that they name: `segments`: within a sequence the numbers start at 0 and never fall. Each document but a sequence's last holds 64 to 800 tokens; one sequence is a single document, and another is made of documents of exactly 64 tokens.
All inputs are finite; a program needn't handle non-finite values.
Results may differ from the reference program's by a relative error of at most 0.024.
Values may be sent and summed in bfloat16 or wider, within the bound.
No kernel may reach another device: no remote copies, remote signals or barrier semaphores. Data moves between devices by JAX's collectives and lax.ppermute only.
A program may use at most 448 MiB of HBM per device.

```python
import math
import jax
import jax.numpy as jnp
from jax import lax

MODEL_WIDTH = 1600
QUERY_HEADS = 25
HEAD_SIZE = 64
KEYVALUE_HEADS = 5
WINDOW = 1024
SH = 50
SP = 64
NS = 16
DI = 3200
FF = 5504
SCAN_BLOCK = 64
LENGTH = 2048
SEQS = 8


def draw_segments(key, part):
    key = jax.random.fold_in(key, 7)
    first_key, second_key = jax.random.split(key)
    shortest = LENGTH // 32
    longest = LENGTH * 25 // 64
    doc_count = LENGTH // shortest + 1
    doc_lengths = jax.random.randint(first_key, (SEQS, doc_count), shortest, longest + 1)
    doc_ends = jnp.cumsum(doc_lengths, axis=1)
    places = jnp.arange(LENGTH, dtype=jnp.int32)
    numbers = jnp.sum((doc_ends[:, None, :] <= places[None, :, None]).astype(jnp.int32), axis=2)
    single = jax.random.randint(second_key, (), 0, SEQS)
    packed = (single + 1) % SEQS
    rows_index = jnp.arange(SEQS)[:, None]
    dense = (places // shortest)[None, :]
    numbers = jnp.where(rows_index == packed, dense, numbers)
    return jnp.where(rows_index == single, 0, numbers).astype(jnp.int32)


def level_of(stream_key, dims, cuts, least, largest):
    def one(dim, shards_of):
        heights = jax.random.uniform(jax.random.fold_in(jax.random.fold_in(stream_key, 6), dim), (shards_of,), jnp.float32, least / len(cuts), largest / len(cuts))
        return jnp.repeat(jnp.exp(heights), dims[dim] // shards_of).reshape((-1,) + (1,) * (len(dims) - dim - 1))

    level = one(*cuts[0])
    for cut in cuts[1:]:
        level = level * one(*cut)
    return level


def normal_values(own_key, dims, deviation, most, cuts=(), kind=jnp.bfloat16):
    values = deviation * jax.random.normal(own_key, dims, jnp.float32)
    if cuts:
        values = values * level_of(own_key, dims, cuts, -0.22, 0.18)
    return jnp.clip(values, -most, most).astype(kind)


def setup_inputs(seed: int = 0) -> dict:
    streams_of = jax.random.split(jax.random.key(seed), 18)
    tokens = normal_values(streams_of[0], (SEQS, LENGTH, MODEL_WIDTH), 1.0, 6.0, ((0, 8), (1, 16)))
    segments = draw_segments(jax.random.fold_in(streams_of[17], 71), 0)
    input_gain = jnp.clip(1.0 + 0.1 * jax.random.normal(streams_of[2], (MODEL_WIDTH,), jnp.float32), 0.5, 1.5).astype(jnp.bfloat16)
    attention_weight = normal_values(streams_of[3], (MODEL_WIDTH, QUERY_HEADS * HEAD_SIZE + 2 * KEYVALUE_HEADS * HEAD_SIZE), MODEL_WIDTH ** -0.5, 0.15625, ((0, 16),))
    attend_out = normal_values(streams_of[4], (QUERY_HEADS * HEAD_SIZE, MODEL_WIDTH), (QUERY_HEADS * HEAD_SIZE) ** -0.5, 0.15625, ((0, 16),))
    mixer_weight = normal_values(streams_of[5], (MODEL_WIDTH, 2 * DI), MODEL_WIDTH ** -0.5, 0.15625, ((0, 16),))
    param_weight = normal_values(streams_of[6], (MODEL_WIDTH, 2 * NS + SH), MODEL_WIDTH ** -0.5, 0.15625, ((0, 16),))
    mixer_out = normal_values(streams_of[7], (DI, MODEL_WIDTH), DI ** -0.5, 0.109375, ((0, 16),))
    attend_gain = jnp.clip(1.0 + 0.1 * jax.random.normal(streams_of[8], (MODEL_WIDTH,), jnp.float32), 0.5, 1.5).astype(jnp.bfloat16)
    mixer_gain = jnp.clip(1.0 + 0.1 * jax.random.normal(streams_of[9], (MODEL_WIDTH,), jnp.float32), 0.5, 1.5).astype(jnp.bfloat16)
    feed_gain = jnp.clip(1.0 + 0.1 * jax.random.normal(streams_of[10], (MODEL_WIDTH,), jnp.float32), 0.5, 1.5).astype(jnp.bfloat16)
    gateup_weight = normal_values(streams_of[11], (MODEL_WIDTH, 2, FF), MODEL_WIDTH ** -0.5, 0.15625, ((2, 16),))
    down_weight = normal_values(streams_of[12], (FF, MODEL_WIDTH), FF ** -0.5, 0.078125, ((0, 16),))
    decay_log = jnp.clip(jax.random.uniform(streams_of[13], (SH,), jnp.float32, -5.3, -0.7), -5.3, -0.7)
    step_bias = jnp.clip(jax.random.uniform(streams_of[14], (SH,), jnp.float32, -3.0, -1.0), -3.0, -1.0)
    skip_gain = jnp.clip(jax.random.uniform(streams_of[15], (SH,), jnp.float32, 0.5, 1.5), 0.5, 1.5)
    cotangent = normal_values(streams_of[16], (SEQS, LENGTH, MODEL_WIDTH), 1.0, 6.0, ((0, 8), (1, 16)))
    return {"tokens": tokens, "segments": segments, "input_gain": input_gain, "attention_weight": attention_weight, "attend_out": attend_out, "mixer_weight": mixer_weight, "param_weight": param_weight, "mixer_out": mixer_out, "attend_gain": attend_gain, "mixer_gain": mixer_gain, "feed_gain": feed_gain, "gateup_weight": gateup_weight, "down_weight": down_weight, "decay_log": decay_log, "step_bias": step_bias, "skip_gain": skip_gain, "cotangent": cotangent}


@jax.custom_vjp
def low(v):
    return lax.optimization_barrier(v.astype(jnp.bfloat16)).astype(jnp.float32)

@jax.custom_vjp
def low_back(v):
    return v

def low_keep(v):
    return (low(v), None)

def low_pass(kept, grad):
    return (grad,)

def back_keep(v):
    return (v, None)

def back_low(kept, grad):
    return (low(grad),)
low.defvjp(low_keep, low_pass)
low_back.defvjp(back_keep, back_low)

def matmul(left, right):
    return jnp.dot(left, right, precision=lax.Precision.HIGHEST)

def root_norm(values, gain):
    return values * lax.rsqrt(lax.optimization_barrier(jnp.mean(values * values, axis=-1, keepdims=True)) + 1e-06) * gain

def attend(query_rows, rows_of_keys, rows_of_values, seg_ids):
    sequence_length = query_rows.shape[0]
    group_width = QUERY_HEADS // KEYVALUE_HEADS
    heads_of_queries = query_rows.reshape(sequence_length, KEYVALUE_HEADS, group_width, HEAD_SIZE)
    heads_of_keys = rows_of_keys.reshape(sequence_length, KEYVALUE_HEADS, HEAD_SIZE)
    heads_of_values = rows_of_values.reshape(sequence_length, KEYVALUE_HEADS, HEAD_SIZE)
    places = jnp.arange(sequence_length, dtype=jnp.int32)
    block_rows = math.gcd(512, sequence_length)

    def one_block(offset):
        block_query = lax.dynamic_slice_in_dim(heads_of_queries, offset, block_rows, 0)
        block_segs = lax.dynamic_slice_in_dim(seg_ids, offset, block_rows, 0)
        block_places = offset + jnp.arange(block_rows, dtype=jnp.int32)
        scores = jnp.einsum('qkgd,skd->kgqs', block_query, heads_of_keys, precision=lax.Precision.HIGHEST) * HEAD_SIZE ** (-0.5)
        scores = low_back(scores)
        allowed = (block_segs[:, None] == seg_ids[None, :]) & (places[None, :] <= block_places[:, None]) & (block_places[:, None] - places[None, :] < WINDOW)
        scores = jnp.where(allowed, scores, -1e+30)
        shifted = jnp.exp(scores - lax.optimization_barrier(jnp.max(scores, axis=-1, keepdims=True)))
        softmax = low(shifted / lax.optimization_barrier(jnp.sum(shifted, axis=-1, keepdims=True)))
        mixed = jnp.einsum('kgqs,skd->qkgd', softmax, heads_of_values, precision=lax.Precision.HIGHEST)
        return mixed.reshape(block_rows, QUERY_HEADS * HEAD_SIZE)
    offsets = jnp.arange(0, sequence_length, block_rows, dtype=jnp.int32)
    return lax.map(jax.checkpoint(one_block), offsets).reshape(sequence_length, QUERY_HEADS * HEAD_SIZE)

def state_pieces(inner, columns, decay_log, step_bias, skip_gain, seg_ids, seg_before):
    count_of_rows = inner.shape[0]
    drive_in = inner[:, :DI].reshape(count_of_rows, SH, SP)
    gates = inner[:, DI:]
    b_rows = columns[:, :NS]
    c_rows = columns[:, NS:2 * NS]
    step = jax.nn.softplus(columns[:, 2 * NS:] + step_bias)
    cumul = jnp.cumsum(-jnp.exp(decay_log) * step, axis=0)
    order = jnp.arange(count_of_rows, dtype=jnp.int32)
    linked = (order[:, None] >= order[None, :]) & (seg_ids[:, None] == seg_ids[None, :])
    linked_heads = linked[:, :, None]
    gaps = jnp.where(linked_heads, cumul[:, None, :] - cumul[None, :, :], 0.0)
    intersection_free = jnp.dot(c_rows, b_rows.T, precision=lax.Precision.HIGHEST)
    kernel = jnp.where(linked_heads, jnp.exp(gaps), 0.0) * intersection_free[:, :, None]
    drive = step[:, :, None] * drive_in
    base = jnp.einsum('ijh,jhp->ihp', kernel, drive, precision=lax.Precision.HIGHEST) + skip_gain[None, :, None] * drive_in
    alive = (seg_ids == seg_before).astype(jnp.float32)
    carry_in = alive[:, None] * jnp.exp(cumul)
    tail_keep = (seg_ids == seg_ids[count_of_rows - 1]).astype(jnp.float32)
    tail = tail_keep[:, None] * jnp.exp(cumul[count_of_rows - 1][None, :] - cumul)
    end_local = jnp.einsum('jh,jhp,jn->hpn', tail, drive, b_rows, precision=lax.Precision.HIGHEST)
    return (base, carry_in, c_rows, gates, end_local, carry_in[count_of_rows - 1])

def state_finish(pieces, entry_state):
    base, carry_in, c_rows, gates, end_local, piece_decay = pieces
    count_of_rows = base.shape[0]
    entered = base + carry_in[:, :, None] * jnp.einsum('in,hpn->ihp', c_rows, entry_state, precision=lax.Precision.HIGHEST)
    result = entered.reshape(count_of_rows, DI) * jax.nn.silu(gates)
    return (result, piece_decay[:, None, None] * entry_state + end_local)

def state_blocks(inner, columns, decay_log, step_bias, skip_gain, seg_ids):
    sequence_length = inner.shape[0]
    block_count = sequence_length // SCAN_BLOCK

    def advance(carried, block_parts):
        entry_state, seg_before = carried
        block_inner, block_columns, block_segs = block_parts
        pieces = state_pieces(block_inner, block_columns, decay_log, step_bias, skip_gain, block_segs, seg_before)
        result, exit_state = state_finish(pieces, entry_state)
        return ((exit_state, block_segs[SCAN_BLOCK - 1]), result)
    start_state = jnp.zeros((SH, SP, NS), jnp.float32)
    block_parts = (inner.reshape(block_count, SCAN_BLOCK, 2 * DI), columns.reshape(block_count, SCAN_BLOCK, 2 * NS + SH), seg_ids.reshape(block_count, SCAN_BLOCK))
    final_carry, results = lax.scan(jax.checkpoint(advance), (start_state, seg_ids[0]), block_parts)
    return results.reshape(sequence_length, DI)

def forward_sequence(tok_in, seg_ids, params):
    input_gain, attention_weight, attend_out, mixer_weight, param_weight, mixer_out, attend_gain, mixer_gain, feed_gain, gateup_weight, down_weight, decay_log, step_bias, skip_gain = params
    normed = low(root_norm(tok_in, input_gain))
    triple = low_back(low(matmul(normed, attention_weight)))
    query_width = QUERY_HEADS * HEAD_SIZE
    keyvalue_width = KEYVALUE_HEADS * HEAD_SIZE
    attended = attend(triple[:, :query_width], triple[:, query_width:query_width + keyvalue_width], triple[:, query_width + keyvalue_width:], seg_ids)
    attended = low_back(low(attended))
    attend_proj = low_back(matmul(attended, attend_out))
    inner = low_back(matmul(normed, mixer_weight))
    columns = low_back(matmul(normed, param_weight))
    mixer_res = low(state_blocks(inner, columns, decay_log, step_bias, skip_gain, seg_ids))
    mixer_proj = low_back(matmul(mixer_res, mixer_out))
    middle = tok_in + root_norm(attend_proj, attend_gain) + root_norm(mixer_proj, mixer_gain)
    feed_in = low(root_norm(middle, feed_gain))
    gate_up = low_back(matmul(feed_in, gateup_weight.reshape(MODEL_WIDTH, 2 * FF)))
    hidden = low(jax.nn.silu(gate_up[:, :FF]) * gate_up[:, FF:])
    return middle + matmul(hidden, down_weight)

def reference(tokens, segments, input_gain, attention_weight, attend_out, mixer_weight, param_weight, mixer_out, attend_gain, mixer_gain, feed_gain, gateup_weight, down_weight, decay_log, step_bias, skip_gain, cotangent):
    params = (input_gain.astype(jnp.float32), attention_weight.astype(jnp.float32), attend_out.astype(jnp.float32), mixer_weight.astype(jnp.float32), param_weight.astype(jnp.float32), mixer_out.astype(jnp.float32), attend_gain.astype(jnp.float32), mixer_gain.astype(jnp.float32), feed_gain.astype(jnp.float32), gateup_weight.astype(jnp.float32), down_weight.astype(jnp.float32), decay_log.astype(jnp.float32), step_bias.astype(jnp.float32), skip_gain.astype(jnp.float32))
    tok_all = tokens.astype(jnp.float32)

    def whole_layer(tok_values, weights):

        def per_sequence(pair):
            return forward_sequence(pair[0], pair[1], weights)
        return lax.map(jax.checkpoint(per_sequence), (tok_values, segments))
    result, pull_back = jax.vjp(whole_layer, tok_all, params)
    grad_tok, grads = pull_back(cotangent.astype(jnp.float32))
    return (result.astype(jnp.bfloat16), grad_tok.astype(jnp.bfloat16), grads[0], grads[1], grads[2], grads[3], grads[4], grads[5], grads[6], grads[7], grads[8], grads[9], grads[10], grads[11], grads[12], grads[13])
```

```python
import jax
import jax.numpy as jnp
from jax import lax
from jax.experimental import pallas as pl
from jax.experimental.pallas import tpu as pltpu
from jax.sharding import Mesh
from jax.sharding import PartitionSpec as P

QUERY_HEADS = 25
HEAD = 64
KV_HEADS = 5
GROUP = 5
WINDOW = 1024
SH = 50
NS = 16
DI = 3200
WIDTH = 1600
FF_ROWS = 344
FF_BLOCK = 136
OUT_BLOCK = 48
RING_ROWS = 192
VMEM_LIMIT = 57 * 1024 * 1024
LENGTH = 2048
PEERS = 16
ROWS = 128
SLOTS = 4
CHUNK = 128
REP = ("z", "yl")
SHARD = ("yh", "x", "core")
SCALE = HEAD**-0.5
IN_WIDTH = 896
BF = jnp.bfloat16
F32 = jnp.float32
HI = lax.Precision.HIGHEST


def mm(a, b, ca=1, cb=0):
    return lax.dot_general(
        a.astype(BF), b.astype(BF), (((ca,), (cb,)), ((), ())), preferred_element_type=F32
    )


def mm32(a, b, ca=1, cb=0):
    return lax.dot_general(
        a, b, (((ca,), (cb,)), ((), ())), precision=HI, preferred_element_type=F32
    )


QB = 256
PARTS = WINDOW // QB + 1
SPAN = QB * PARTS
BLOCKS = LENGTH // QB


def key_parts(step):
    blocks = [step - (PARTS - 1) + j for j in range(PARTS)]
    starts = [pl.multiple_of(jnp.maximum(block, 0) * QB, QB) for block in blocks]
    return starts, [jnp.where(block < 0, 1024, 0) for block in blocks]


def allowed_parts(key_segs, query_segs, starts, missing):
    key = lax.broadcasted_iota(jnp.int32, (QB, QB), 0)
    query = lax.broadcasted_iota(jnp.int32, (QB, QB), 1)
    masks = []
    for j in range(PARTS):
        mask = key_segs[pl.ds(starts[j], QB), :] + missing[j] == query_segs
        if j == 0:
            mask = mask & (key > query)
        if j == PARTS - 1:
            mask = mask & (key <= query)
        masks.append(mask)
    return masks


def scaled(q):
    return (q.astype(BF).astype(F32) * SCALE).astype(BF)


def attend_kernel(q_ref, kv_ref, kvt_ref, key_segs, query_segs, out_ref, log_ref):
    starts, missing = key_parts(pl.program_id(0))
    masks = allowed_parts(key_segs, query_segs[...], starts, missing)
    for h in range(2):
        q = scaled(q_ref[:, HEAD * h : HEAD * (h + 1)])
        scores = []
        for j in range(PARTS):
            s = mm(kv_ref[pl.ds(starts[j], QB), :HEAD], q, 1, 1)
            scores.append(jnp.where(masks[j], s, -1e30))
        top = scores[0]
        for s in scores[1:]:
            top = jnp.maximum(top, s)
        top = jnp.max(top, axis=0, keepdims=True)
        shifted = [jnp.exp(s - top) for s in scores]
        total = shifted[0]
        for s in shifted[1:]:
            total = total + s
        total = jnp.sum(total, axis=0, keepdims=True)
        inverse = 1.0 / total
        out = jnp.zeros((HEAD, QB), F32)
        for j in range(PARTS):
            soft = (shifted[j] * inverse).astype(BF)
            out = out + mm(kvt_ref[HEAD:, pl.ds(starts[j], QB)], soft)
        for c in range(2):
            out_ref[0, c, 0, HEAD * h : HEAD * (h + 1), :] = out[:, ROWS * c : ROWS * (c + 1)].astype(BF)
        log_ref[h : h + 1, :] = top + jnp.log(total)


def attend_back_kernel(
    q_ref, g_ref, kv_ref, kvt_ref, key_segs, query_segs, log_ref, dq_ref, dkv_ref, dk_acc, dv_acc
):
    step = pl.program_id(0)
    starts, missing = key_parts(step)

    @pl.when(step == 0)
    def _():
        dk_acc[...] = jnp.zeros_like(dk_acc)
        dv_acc[...] = jnp.zeros_like(dv_acc)

    masks = allowed_parts(key_segs, query_segs[...], starts, missing)
    g_t = jnp.concatenate([g_ref[0, 0, 0], g_ref[0, 1, 0]], axis=1)
    g_all = g_t.astype(F32).T.astype(BF)
    dqs = []
    for h in range(2):
        q = scaled(q_ref[:, HEAD * h : HEAD * (h + 1)])
        g = g_all[:, HEAD * h : HEAD * (h + 1)]
        log_total = log_ref[h : h + 1, :]
        softs, grads = [], []
        delta = jnp.zeros((QB, QB), F32)
        for j in range(PARTS):
            rows = pl.ds(starts[j], QB)
            s = mm(kv_ref[rows, :HEAD], q, 1, 1)
            soft = jnp.exp(jnp.where(masks[j], s - log_total, -1e30))
            d_soft = mm(kv_ref[rows, HEAD:], g_t[HEAD * h : HEAD * (h + 1), :])
            delta = delta + soft * d_soft
            dv_acc[rows, :] += mm(soft, g)
            softs.append(soft)
            grads.append(d_soft)
        delta = jnp.sum(delta, axis=0, keepdims=True)
        dq = jnp.zeros((HEAD, QB), F32)
        for j in range(PARTS):
            rows = pl.ds(starts[j], QB)
            d_scores = (softs[j] * (grads[j] - delta)).astype(BF)
            dk_acc[rows, :] += mm(d_scores, q)
            dq = dq + mm(kvt_ref[:HEAD, rows], d_scores)
        dqs.append(dq * SCALE)
    dq_ref[...] = jnp.concatenate(dqs, axis=0).T.astype(BF)

    @pl.when(step == BLOCKS - 1)
    def _():
        dkv_ref[...] = jnp.concatenate([dk_acc[...], dv_acc[...]], axis=1).astype(BF)


def whole(*shape):
    return pl.BlockSpec(shape, lambda i: (0,) * len(shape))


def attend(projected, kv, kvt, key_segs, query_segs):
    return pl.pallas_call(
        attend_kernel,
        grid=(BLOCKS,),
        in_specs=[
            pl.BlockSpec((QB, 128), lambda i: (i, 0)),
            whole(LENGTH, 128),
            whole(128, LENGTH),
            whole(LENGTH, 1),
            pl.BlockSpec((1, QB), lambda i: (0, i)),
        ],
        out_specs=[
            pl.BlockSpec((1, 2, 1, 128, ROWS), lambda i: (i // 4, 0, i % 4, 0, 0)),
            pl.BlockSpec((8, QB), lambda i: (0, i)),
        ],
        out_shape=[
            jax.ShapeDtypeStruct((2, 2, 4, 128, ROWS), BF),
            jax.ShapeDtypeStruct((8, LENGTH), F32),
        ],
        compiler_params=pltpu.CompilerParams(vmem_limit_bytes=VMEM_LIMIT),
        cost_estimate=pl.CostEstimate(
            flops=10_000_000_000, bytes_accessed=4_000_000, transcendentals=5_300_000
        ),
        name="attend",
    )(projected, kv, kvt, key_segs, query_segs)


def attend_back(projected, g, kv, kvt, key_segs, query_segs, logs):
    return pl.pallas_call(
        attend_back_kernel,
        grid=(BLOCKS,),
        in_specs=[
            pl.BlockSpec((QB, 128), lambda i: (i, 0)),
            pl.BlockSpec((1, 2, 1, 128, ROWS), lambda i: (i // 4, 0, i % 4, 0, 0)),
            whole(LENGTH, 128),
            whole(128, LENGTH),
            whole(LENGTH, 1),
            pl.BlockSpec((1, QB), lambda i: (0, i)),
            pl.BlockSpec((8, QB), lambda i: (0, i)),
        ],
        out_specs=[
            pl.BlockSpec((QB, 128), lambda i: (i, 0)),
            whole(LENGTH, 128),
        ],
        out_shape=[
            jax.ShapeDtypeStruct((LENGTH, 128), BF),
            jax.ShapeDtypeStruct((LENGTH, 128), BF),
        ],
        scratch_shapes=[
            pltpu.VMEM((LENGTH, HEAD), F32),
            pltpu.VMEM((LENGTH, HEAD), F32),
        ],
        compiler_params=pltpu.CompilerParams(vmem_limit_bytes=VMEM_LIMIT),
        cost_estimate=pl.CostEstimate(
            flops=25_000_000_000, bytes_accessed=5_000_000, transcendentals=5_300_000
        ),
        name="attend_back",
    )(projected, g, kv, kvt, key_segs, query_segs, logs)


LANES = SLOTS * 64
CHUNKS = LENGTH // CHUNK
PAIR = 2
STEP = PAIR * CHUNK
STEPS = LENGTH // STEP


def head_selector(transposed=False):
    shape = (LANES, 8) if transposed else (8, LANES)
    head = lax.broadcasted_iota(jnp.int32, shape, 1 if transposed else 0)
    lane = lax.broadcasted_iota(jnp.int32, shape, 0 if transposed else 1)
    return (lane // 64 == head).astype(F32)


def softplus(v):
    return jnp.maximum(v, 0.0) + jnp.log1p(jnp.exp(-jnp.abs(v)))


def chunk_values(u, x_ref, bcr_ref, flags_ref, seg_col, seg_row, par_ref):
    rows = slice(CHUNK * u, CHUNK * (u + 1))
    row = lax.broadcasted_iota(jnp.int32, (CHUNK, CHUNK), 0)
    col = lax.broadcasted_iota(jnp.int32, (CHUNK, CHUNK), 1)
    linked = (row >= col) & (seg_col[rows, :] == seg_row[:, rows])
    b, c = bcr_ref[rows, :NS], bcr_ref[rows, NS : 2 * NS]
    raw = bcr_ref[rows, 2 * NS : 2 * NS + 8] + par_ref[1:2, :]
    step = softplus(raw)
    logs = step * par_ref[0:1, :]
    cum = mm32((row >= col).astype(F32), logs)
    carry = flags_ref[rows, 0:1] * jnp.exp(cum)
    tail = flags_ref[rows, 1:2] * jnp.exp(cum[CHUNK - 1 : CHUNK, :] - cum)
    wide = mm32(jnp.concatenate([step, carry, tail], axis=0), head_selector())
    step_w, carry_w, tail_w = wide[:CHUNK], wide[CHUNK : 2 * CHUNK], wide[2 * CHUNK :]
    cum_t = cum.T
    inner = mm32(c, b, 1, 1)
    decays = []
    for h in range(SLOTS):
        gap = jnp.minimum(cum[:, h : h + 1] - cum_t[h : h + 1, :], 0.0)
        decays.append(jnp.where(linked, jnp.exp(gap), 0.0))
    drive = step_w * x_ref[rows, :]
    return b, c, raw, step, logs, step_w, carry_w, tail_w, inner, decays, drive


def by_head(values):
    selector = head_selector()
    return [(values * selector[h : h + 1, :]).astype(BF) for h in range(SLOTS)]


def state_kernel(
    x_ref, z_ref, bcr_ref, flags_ref, seg_col, seg_row, par_ref, skip_ref, mixed_ref, y_ref, entry_ref, state
):
    @pl.when(pl.program_id(0) == 0)
    def _():
        state[...] = jnp.zeros_like(state)

    entry = state[...]
    for u in range(PAIR):
        rows = slice(CHUNK * u, CHUNK * (u + 1))
        b, c, _, _, _, _, carry_w, tail_w, inner, decays, drive = chunk_values(
            u, x_ref, bcr_ref, flags_ref, seg_col, seg_row, par_ref
        )
        kernels = jnp.concatenate([(d * inner).astype(BF) for d in decays], axis=1)
        drives = jnp.concatenate(by_head(drive), axis=0)
        y = mm(kernels, drives) + skip_ref[...] * x_ref[rows, :]
        ends = mm(b, tail_w * drive, 0, 0)
        entry_ref[u] = entry
        y = y + carry_w * mm(c, entry)
        entry = carry_w[CHUNK - 1 : CHUNK, :] * entry + ends
        y_ref[rows, :] = y
        z = z_ref[rows, :]
        mixed_ref[0, u, 0] = (y * z * jax.nn.sigmoid(z)).T.astype(BF)
    state[...] = entry


def state_back_kernel(
    x_ref,
    z_ref,
    bcr_ref,
    flags_ref,
    seg_col,
    seg_row,
    par_ref,
    skip_ref,
    y_ref,
    entry_ref,
    g_ref,
    dx_ref,
    dz_ref,
    dbcr_ref,
    dpar_ref,
    dskip_ref,
    d_state,
):
    @pl.when(pl.program_id(0) == 0)
    def _():
        d_state[...] = jnp.zeros_like(d_state)
        dpar_ref[...] = jnp.zeros_like(dpar_ref)
        dskip_ref[...] = jnp.zeros_like(dskip_ref)

    d_exit = d_state[...]
    for u in reversed(range(PAIR)):
        rows = slice(CHUNK * u, CHUNK * (u + 1))
        b, c, raw, step, logs, step_w, carry_w, tail_w, inner, decays, drive = chunk_values(
            u, x_ref, bcr_ref, flags_ref, seg_col, seg_row, par_ref
        )
        x, z = x_ref[rows, :], z_ref[rows, :]
        g = g_ref[0, u, 0].astype(F32).T
        sig = jax.nn.sigmoid(z)
        dy = g * z * sig
        dz_ref[rows, :] = (g * y_ref[rows, :] * (sig * (1.0 + z * (1.0 - sig)))).astype(BF)
        entry = entry_ref[u]
        c_entry = mm(c, entry)
        carried = carry_w * dy
        tailed = tail_w * drive
        piece = carry_w[CHUNK - 1 : CHUNK, :]
        dys = by_head(dy)
        kernels, cols = [], []
        row_sums = jnp.zeros((CHUNK, 8), F32)
        d_inner = jnp.zeros((CHUNK, CHUNK), F32)
        place = lax.broadcasted_iota(jnp.int32, (CHUNK, 8), 1)
        drive_low = drive.astype(BF)
        for h in range(SLOTS):
            kernel = decays[h] * inner
            d_kernel = mm(dys[h], drive_low, 1, 1)
            d_inner = d_inner + decays[h] * d_kernel
            d_gap = kernel * d_kernel
            row_sums = row_sums + jnp.where(place == h, jnp.sum(d_gap, axis=1, keepdims=True), 0.0)
            cols.append(jnp.sum(d_gap, axis=0, keepdims=True))
            kernels.append(kernel.astype(BF))
        cols = jnp.concatenate(cols + [jnp.zeros((8 - SLOTS, CHUNK), F32)], axis=0).T
        d_drive = mm(jnp.concatenate(kernels, axis=0), jnp.concatenate(dys, axis=0), 0, 0)
        b_exit = mm(b, d_exit)
        d_drive = d_drive + tail_w * b_exit
        dx_ref[rows, :] = (step_w * d_drive + skip_ref[...] * dy).astype(BF)
        dskip_ref[...] += jnp.sum(dy * x, axis=0, keepdims=True)
        ends = jnp.sum(entry * d_exit, axis=0, keepdims=True) * piece
        sums = mm32(
            jnp.concatenate(
                [d_drive * x, carried * c_entry, tailed * b_exit, jnp.broadcast_to(ends, (8, LANES))], axis=0
            ),
            head_selector(True),
        )
        d_step, from_carry, from_tail = sums[:CHUNK], sums[CHUNK : 2 * CHUNK], sums[2 * CHUNK : 3 * CHUNK]
        d_last = jnp.sum(from_tail, axis=0, keepdims=True) + sums[3 * CHUNK : 3 * CHUNK + 1]
        d_cum = row_sums - cols + from_carry - from_tail
        row = lax.broadcasted_iota(jnp.int32, (CHUNK, CHUNK), 0)
        col = lax.broadcasted_iota(jnp.int32, (CHUNK, CHUNK), 1)
        d_logs = mm32((row <= col).astype(F32), d_cum) + d_last
        d_step = d_step + d_logs * par_ref[0:1, :]
        d_raw = d_step * jax.nn.sigmoid(raw)
        dpar_ref[0:1, :] += jnp.sum(d_logs * logs, axis=0, keepdims=True)
        dpar_ref[1:2, :] += jnp.sum(d_raw, axis=0, keepdims=True)
        d_b = mm(d_inner, c, 0, 0) + mm(tailed, d_exit, 1, 1)
        d_c = mm(d_inner, b) + mm(carried, entry, 1, 1)
        dbcr_ref[rows, :] = jnp.concatenate(
            [d_b, d_c, d_raw, jnp.zeros((CHUNK, 128 - 2 * NS - 8), F32)], axis=1
        ).astype(BF)
        d_exit = piece * d_exit + mm(c, carried, 0, 0)
    d_state[...] = d_exit


def owner_block(place):
    return pl.BlockSpec(
        (1, PAIR, 1, LANES, CHUNK), lambda i: (place(i) // 4, 0, place(i) % 4, 0, 0)
    )


def state_specs(place):
    return [
        pl.BlockSpec((STEP, LANES), lambda i: (place(i), 1)),
        pl.BlockSpec((STEP, LANES), lambda i: (place(i), 2)),
        pl.BlockSpec((STEP, 128), lambda i: (place(i), 6)),
        pl.BlockSpec((STEP, 2), lambda i: (place(i), 0)),
        pl.BlockSpec((STEP, 1), lambda i: (place(i), 0)),
        pl.BlockSpec((1, STEP), lambda i: (0, place(i))),
        pl.BlockSpec((2, 8), lambda i: (0, 0)),
        pl.BlockSpec((1, LANES), lambda i: (0, 0)),
    ]


def states(projected, flags, seg_col, seg_row, par, skip):
    return pl.pallas_call(
        state_kernel,
        grid=(STEPS,),
        in_specs=state_specs(lambda i: i),
        out_specs=[
            owner_block(lambda i: i),
            pl.BlockSpec((STEP, LANES), lambda i: (i, 0)),
            pl.BlockSpec((PAIR, NS, LANES), lambda i: (i, 0, 0)),
        ],
        out_shape=[
            jax.ShapeDtypeStruct((2, 2, 4, LANES, CHUNK), BF),
            jax.ShapeDtypeStruct((LENGTH, LANES), F32),
            jax.ShapeDtypeStruct((CHUNKS, NS, LANES), F32),
        ],
        scratch_shapes=[pltpu.VMEM((NS, LANES), F32)],
        compiler_params=pltpu.CompilerParams(vmem_limit_bytes=VMEM_LIMIT),
        cost_estimate=pl.CostEstimate(flops=1_500_000_000, bytes_accessed=10_000_000, transcendentals=2_000_000),
        name="states",
    )(projected, projected, projected, flags, seg_col, seg_row, par, skip)


def states_back(projected, flags, seg_col, seg_row, par, skip, y, entry, g):
    def back(i):
        return STEPS - 1 - i

    return pl.pallas_call(
        state_back_kernel,
        grid=(STEPS,),
        in_specs=state_specs(back)
        + [
            pl.BlockSpec((STEP, LANES), lambda i: (back(i), 0)),
            pl.BlockSpec((PAIR, NS, LANES), lambda i: (back(i), 0, 0)),
            owner_block(back),
        ],
        out_specs=[
            pl.BlockSpec((STEP, LANES), lambda i: (back(i), 0)),
            pl.BlockSpec((STEP, LANES), lambda i: (back(i), 0)),
            pl.BlockSpec((STEP, 128), lambda i: (back(i), 0)),
            pl.BlockSpec((2, 8), lambda i: (0, 0)),
            pl.BlockSpec((1, LANES), lambda i: (0, 0)),
        ],
        out_shape=[
            jax.ShapeDtypeStruct((LENGTH, LANES), BF),
            jax.ShapeDtypeStruct((LENGTH, LANES), BF),
            jax.ShapeDtypeStruct((LENGTH, 128), BF),
            jax.ShapeDtypeStruct((2, 8), F32),
            jax.ShapeDtypeStruct((1, LANES), F32),
        ],
        scratch_shapes=[pltpu.VMEM((NS, LANES), F32)],
        compiler_params=pltpu.CompilerParams(vmem_limit_bytes=VMEM_LIMIT),
        cost_estimate=pl.CostEstimate(flops=4_000_000_000, bytes_accessed=12_000_000, transcendentals=3_000_000),
        name="states_back",
    )(projected, projected, projected, flags, seg_col, seg_row, par, skip, y, entry, g)


def once(*shape):
    return pl.BlockSpec(shape, lambda i: (0,) * len(shape), pipeline_mode=pl.Buffered(1))


def place_kernel(where_ref, *refs):
    *blocks, out_ref = refs
    for h in range(2):
        near, right, far_top, far_low, left = blocks[5 * h : 5 * h + 5]
        half = lax.rem(where_ref[0] + h, 2) * 4
        spots = [half + lax.rem(where_ref[1] + k, 4) for k in range(4)]
        out_ref[spots[0]] = near[...]
        out_ref[spots[1]] = right[...]
        out_ref[spots[2], :64] = far_top[...]
        out_ref[spots[2], 64:] = far_low[...]
        out_ref[spots[3]] = left[...]


def place(where, blocks):
    return pl.pallas_call(
        place_kernel,
        grid=(1,),
        in_specs=[pl.BlockSpec(memory_space=pltpu.SMEM)] + [once(*v.shape) for v in blocks],
        out_specs=once(8, ROWS + 16, WIDTH),
        out_shape=jax.ShapeDtypeStruct((8, ROWS + 16, WIDTH), BF),
        compiler_params=pltpu.CompilerParams(vmem_limit_bytes=VMEM_LIMIT),
        cost_estimate=pl.CostEstimate(flops=0, bytes_accessed=9_000_000, transcendentals=0),
        name="place",
    )(where, *blocks)


def spread_kernel(attention_ref, mixer_ref, param_ref, out_ref):
    attention, mixer, param = attention_ref[...], mixer_ref[...], param_ref[...]

    def empty(width):
        return jnp.zeros((100, width), BF)

    for s in range(PEERS):
        group, pair = s // 3, s % 3
        if s == 15:
            parts = [empty(256)]
        else:
            at = 64 * (5 * group + 2 * pair)
            width = 128 if pair < 2 else 64
            parts = [attention[:, at : at + width]] + [empty(128 - width)] * (pair == 2)
            parts += [attention[:, at : at + 64] for at in (1600 + 64 * group, 1920 + 64 * group)]
        for side in (0, DI):
            parts.append(mixer[:, side + 192 * s : side + 192 * (s + 1)])
            at = side + 48 * 64 + 64 * s
            parts.append(mixer[:, at : at + 64] if s < 2 else empty(64))
        parts += [param[:, : 2 * NS], param[:, 2 * NS + 3 * s : 2 * NS + 3 * (s + 1)]]
        parts.append(param[:, 80 + s : 81 + s] if s < 2 else empty(1))
        parts.append(empty(128 - 2 * NS - SLOTS))
        out_ref[s] = jnp.concatenate(parts, axis=1)


def spread_inputs(attention, mixer, param):
    return pl.pallas_call(
        spread_kernel,
        grid=(1,),
        in_specs=[once(*v.shape) for v in (attention, mixer, param)],
        out_specs=once(PEERS, 100, IN_WIDTH),
        out_shape=jax.ShapeDtypeStruct((PEERS, 100, IN_WIDTH), BF),
        compiler_params=pltpu.CompilerParams(vmem_limit_bytes=VMEM_LIMIT),
        cost_estimate=pl.CostEstimate(flops=0, bytes_accessed=5_000_000, transcendentals=0),
        name="spread",
    )(attention, mixer, param)


def in_order(core, mine, other):
    first = jnp.where(core == 0, mine, other)
    second = jnp.where(core == 0, other, mine)
    return first, second


def project_kernel(core_ref, mine_ref, other_ref, gain_ref, weight_ref, normed_ref, out_ref, kv_ref, kvt_ref):
    mine, other = mine_ref[0, :ROWS, :].astype(F32), other_ref[0, :ROWS, :].astype(F32)
    tok = jnp.concatenate(in_order(core_ref[0], mine, other), axis=0)
    scale = lax.rsqrt(jnp.mean(tok * tok, axis=-1, keepdims=True) + 1e-06)
    normed = (tok * scale * gain_ref[...]).astype(BF)
    normed_ref[...] = normed
    projected = mm(normed, weight_ref[...])
    out_ref[...] = projected
    kv = projected[:, 128:256]
    kv_ref[...] = kv.astype(BF)
    kvt_ref[...] = kv.T.astype(BF)


def project(core, mine, other, gain, weight):
    return pl.pallas_call(
        project_kernel,
        grid=(8,),
        in_specs=[
            pl.BlockSpec(memory_space=pltpu.SMEM),
            pl.BlockSpec((1, ROWS + 16, WIDTH), lambda i: (i, 0, 0)),
            pl.BlockSpec((1, ROWS + 16, WIDTH), lambda i: (i, 0, 0)),
            once(1, WIDTH),
            once(WIDTH, IN_WIDTH),
        ],
        out_specs=[
            pl.BlockSpec((2 * ROWS, WIDTH), lambda i: (i, 0)),
            pl.BlockSpec((2 * ROWS, IN_WIDTH), lambda i: (i, 0)),
            pl.BlockSpec((2 * ROWS, 128), lambda i: (i, 0)),
            pl.BlockSpec((128, 2 * ROWS), lambda i: (0, i)),
        ],
        out_shape=[
            jax.ShapeDtypeStruct((LENGTH, WIDTH), BF),
            jax.ShapeDtypeStruct((LENGTH, IN_WIDTH), F32),
            jax.ShapeDtypeStruct((LENGTH, 128), BF),
            jax.ShapeDtypeStruct((128, LENGTH), BF),
        ],
        compiler_params=pltpu.CompilerParams(vmem_limit_bytes=VMEM_LIMIT),
        cost_estimate=pl.CostEstimate(
            flops=8_000_000_000, bytes_accessed=24_000_000, transcendentals=0
        ),
        name="project",
    )(core, mine, other, gain, weight)


def store_parts(refs, values):
    for ref, (start, stop) in zip(refs, ((0, 128), (128, 256), (256, 320), (320, 384), (384, 512))):
        ref[...] = values[start:stop].astype(BF)


def feed_kernel(*refs):
    feeds, grads, gate_ups, downs = refs[:5], refs[5:10], refs[10:14], refs[14:18]
    feed_ref, grad_ref, hidden_ref, d_gate_up_ref = refs[18:22]
    for parts, target in ((feeds, feed_ref), (grads, grad_ref)):
        at = 0
        for part in parts:
            target[at : at + part.shape[0], :] = part[...]
            at += part.shape[0]
    feed, grad = feed_ref[...], grad_ref[...]
    out = jnp.zeros((512, WIDTH), F32)
    d_feed = jnp.zeros((512, WIDTH), F32)
    for b in range(4):
        gate_up = mm(feed, gate_ups[b][...], 1, 1)
        d_hidden = mm(grad, downs[b][...], 1, 1)
        gate, up = gate_up[:, :FF_ROWS], gate_up[:, FF_ROWS:]
        sigmoid = jax.nn.sigmoid(gate)
        silu = gate * sigmoid
        hidden = (silu * up).astype(BF)
        d_gate = d_hidden * up * (sigmoid * (1.0 + gate * (1.0 - sigmoid)))
        d_gate_up = jnp.concatenate([d_gate, d_hidden * silu], axis=1).astype(BF)
        hidden_ref[b] = hidden
        d_gate_up_ref[b] = d_gate_up
        out = out + mm(hidden, downs[b][...])
        d_feed = d_feed + mm(d_gate_up, gate_ups[b][...])
    store_parts(refs[22:27], out)
    store_parts(refs[27:32], d_feed)


def feed_forward(feeds, grads, gate_ups, downs):
    parts = [(ROWS, WIDTH), (ROWS, WIDTH), (64, WIDTH), (64, WIDTH), (ROWS, WIDTH)]
    shapes = [(512, WIDTH)] * 2 + [(4, 512, FF_ROWS), (4, 512, 2 * FF_ROWS)] + parts + parts
    return pl.pallas_call(
        feed_kernel,
        grid=(1,),
        in_specs=[once(*v.shape) for v in (*feeds, *grads, *gate_ups, *downs)],
        out_specs=[once(*shape) for shape in shapes],
        out_shape=[jax.ShapeDtypeStruct(shape, BF) for shape in shapes],
        compiler_params=pltpu.CompilerParams(vmem_limit_bytes=VMEM_LIMIT),
        cost_estimate=pl.CostEstimate(
            flops=25_000_000_000, bytes_accessed=28_000_000, transcendentals=700_000
        ),
        name="feed_forward",
    )(*feeds, *grads, *gate_ups, *downs)


def feed_grads_kernel(feed_ref, grad_ref, hidden_ref, d_gate_up_ref, near_ref, far_ref):
    for b, out_ref in enumerate((near_ref, far_ref)):
        gate_up = mm(d_gate_up_ref[b], feed_ref[...], 0, 0)
        down = mm(hidden_ref[b], grad_ref[...], 0, 0)
        empty = jnp.zeros((8 * FF_BLOCK - 3 * FF_ROWS, WIDTH), F32)
        together = jnp.concatenate([gate_up, down, empty], axis=0).astype(BF)
        for i in range(8):
            out_ref[i] = together[FF_BLOCK * i : FF_BLOCK * (i + 1)]


def feed_grads(half, feed, grad, hidden, d_gate_up):
    return pl.pallas_call(
        feed_grads_kernel,
        grid=(1,),
        in_specs=[
            once(512, WIDTH),
            once(512, WIDTH),
            pl.BlockSpec((2, 512, FF_ROWS), lambda i: (half, 0, 0), pipeline_mode=pl.Buffered(1)),
            pl.BlockSpec((2, 512, 2 * FF_ROWS), lambda i: (half, 0, 0), pipeline_mode=pl.Buffered(1)),
        ],
        out_specs=[once(8, FF_BLOCK, WIDTH)] * 2,
        out_shape=[jax.ShapeDtypeStruct((8, FF_BLOCK, WIDTH), BF)] * 2,
        compiler_params=pltpu.CompilerParams(vmem_limit_bytes=VMEM_LIMIT),
        cost_estimate=pl.CostEstimate(
            flops=5_000_000_000, bytes_accessed=12_000_000, transcendentals=0
        ),
        name="feed_grads",
    )(feed, grad, hidden, d_gate_up)


def in_grads_kernel(normed_ref, *refs):
    *parts, weight_ref, small_ref, out_ref, acc = refs
    step = pl.program_id(0)

    @pl.when(step == 0)
    def _():
        acc[...] = jnp.zeros_like(acc)

    acc[...] += mm(normed_ref[...], jnp.concatenate([part[...] for part in parts], axis=1), 0, 0)

    @pl.when(step == 7)
    def _():
        width = acc.shape[1]
        product = acc[...] * weight_ref[...].astype(F32)
        gain = mm32(jnp.ones((8, width), F32), product, 1, 1)[:1]
        for s in range(PEERS):
            own_gain = jnp.pad(gain[:, 100 * s : 100 * (s + 1)], ((0, 0), (width - 128, 28)))
            out_ref[s] = jnp.concatenate(
                [acc[100 * s : 100 * (s + 1), :], small_ref[s : s + 1, :] + own_gain, jnp.zeros((3, width), F32)],
                axis=0,
            ).astype(BF)


def projected_specs():
    return [
        pl.BlockSpec((256, 128), lambda i: (i, 0)),
        pl.BlockSpec((256, 128), lambda i: (i, 0)),
        pl.BlockSpec((256, 256), lambda i: (i, 0)),
        pl.BlockSpec((256, 256), lambda i: (i, 0)),
        pl.BlockSpec((256, 128), lambda i: (i, 0)),
    ]


def in_grads(normed, parts, weight, small):
    width = weight.shape[1]
    return pl.pallas_call(
        in_grads_kernel,
        grid=(8,),
        in_specs=[pl.BlockSpec((256, WIDTH), lambda i: (i, 0))]
        + [pl.BlockSpec((256, part.shape[1]), lambda i: (i, 0)) for part in parts]
        + [once(WIDTH, width), once(PEERS, width)],
        out_specs=once(PEERS, 104, width),
        out_shape=jax.ShapeDtypeStruct((PEERS, 104, width), BF),
        scratch_shapes=[pltpu.VMEM((WIDTH, width), F32)],
        compiler_params=pltpu.CompilerParams(vmem_limit_bytes=VMEM_LIMIT),
        cost_estimate=pl.CostEstimate(
            flops=10 * LENGTH * width * 1000, bytes_accessed=14_000_000, transcendentals=0
        ),
        name="in_grads",
    )(normed, *parts, weight, small)


def d_normed_kernel(core_ref, q_ref, kv_ref, x_ref, z_ref, bcr_ref, weight_ref, kept_ref, sent_ref):
    parts = [q_ref[...], kv_ref[...], x_ref[...], z_ref[...], bcr_ref[...]]
    d_normed = mm(jnp.concatenate(parts, axis=1), weight_ref[...], 1, 1)
    kept, sent = in_order(core_ref[0], d_normed[:ROWS], d_normed[ROWS:])
    kept_ref[0] = kept.astype(BF)
    sent_ref[0] = sent.astype(BF)


def d_normed_parts(core, d_parts, weight):
    return pl.pallas_call(
        d_normed_kernel,
        grid=(8,),
        in_specs=[pl.BlockSpec(memory_space=pltpu.SMEM)] + projected_specs() + [once(WIDTH, IN_WIDTH)],
        out_specs=[pl.BlockSpec((1, ROWS, WIDTH), lambda i: (i, 0, 0))] * 2,
        out_shape=[jax.ShapeDtypeStruct((8, ROWS, WIDTH), BF)] * 2,
        compiler_params=pltpu.CompilerParams(vmem_limit_bytes=VMEM_LIMIT),
        cost_estimate=pl.CostEstimate(
            flops=8_000_000_000, bytes_accessed=13_000_000, transcendentals=0
        ),
        name="d_normed",
    )(core, *d_parts, weight)


def rep_spots(z_ref, pieces):
    near, right, far_top, far_low, left = pieces
    spots = [2 * lax.rem(z_ref[0] + k, 4) for k in range(4)]
    pairs = [(spots[0], near), (spots[1], right), (spots[3], left)]
    single = [(spots[2], far_top[...]), (spots[2] + 1, far_low[...])]
    return single + [(spot + yl, pair[yl]) for spot, pair in pairs for yl in range(2)]


def collect_kernel(z_ref, *refs):
    pieces, refs = refs[:5], refs[5:]
    heads_ref, attention_ref, mixer_ref, param_ref, low_states_ref, low_heads_ref, states_ref = refs
    for spot, block in rep_spots(z_ref, pieces):
        for i in range(2):
            states_ref[2 * spot + i] = block[i]
    shared = jnp.zeros((104, 128), F32)
    low_states_ref[...] = jnp.zeros_like(low_states_ref)
    low_heads_ref[...] = jnp.zeros_like(low_heads_ref)
    for s in range(PEERS):
        tile = heads_ref[s].astype(F32)
        low_heads_ref[s : s + 1, :] = tile[100:101, :]
        if s < 15:
            width = 128 if s % 3 < 2 else 64
            at = 64 * (5 * (s // 3) + 2 * (s % 3))
            attention_ref[:, at : at + width] = tile[:100, :width]
        tile = states_ref[s].astype(F32)
        low_states_ref[s : s + 1, :] = tile[100:101, :]
        for side in range(2):
            part = tile[:100, 256 * side : 256 * (side + 1)]
            at = DI * side + 192 * s
            mixer_ref[:, at : at + 192] = part[:, :192]
            if s < 2:
                at = DI * side + 48 * 64 + 64 * s
                mixer_ref[:, at : at + 64] = part[:, 192:]
        raw = tile[:, 512:]
        shared = shared + raw
        at = 2 * NS + 3 * s
        param_ref[:, at : at + 3] = raw[:100, 2 * NS : 2 * NS + 3]
        if s < 2:
            param_ref[:, 80 + s : 81 + s] = raw[:100, 2 * NS + 3 : 2 * NS + 4]
    param_ref[:, : 2 * NS] = shared[:100, : 2 * NS]
    for k in range(KV_HEADS):
        kv = sum(heads_ref[3 * k + j].astype(F32)[:100, 128:] for j in range(3))
        attention_ref[:, 1600 + 64 * k : 1664 + 64 * k] = kv[:, :64]
        attention_ref[:, 1920 + 64 * k : 1984 + 64 * k] = kv[:, 64:]


def collect(z, states_pieces, heads_rows):
    return pl.pallas_call(
        collect_kernel,
        grid=(1,),
        in_specs=[pl.BlockSpec(memory_space=pltpu.SMEM)]
        + [once(*v.shape) for v in (*states_pieces, heads_rows)],
        out_specs=[once(100, 2240), once(100, 2 * DI), once(100, 82), once(PEERS, 640), once(PEERS, 256)],
        out_shape=[
            jax.ShapeDtypeStruct((100, 2240), F32),
            jax.ShapeDtypeStruct((100, 2 * DI), F32),
            jax.ShapeDtypeStruct((100, 82), F32),
            jax.ShapeDtypeStruct((PEERS, 640), F32),
            jax.ShapeDtypeStruct((PEERS, 256), F32),
        ],
        scratch_shapes=[pltpu.VMEM((PEERS, 104, 640), BF)],
        compiler_params=pltpu.CompilerParams(vmem_limit_bytes=VMEM_LIMIT),
        cost_estimate=pl.CostEstimate(flops=0, bytes_accessed=7_000_000, transcendentals=0),
        name="collect",
    )(z, *states_pieces, heads_rows)


def line_tokens(act, source, x):
    return jnp.concatenate([act[source, lax.rem(x + k, 4)] for k in range(4)], axis=1)


def out_kernel(where_ref, att_ref, mix_ref, w00, w01, w10, w11, *outs):
    att = jnp.zeros((512, WIDTH), F32)
    mix = jnp.zeros((512, WIDTH), F32)
    for a, b, weight in ((0, 0, w00), (0, 1, w01), (1, 0, w10), (1, 1, w11)):
        source = lax.rem(where_ref[0] + a, 2) * 2 + lax.rem(where_ref[2] + b, 2)
        mix = mix + mm(line_tokens(mix_ref, source, where_ref[1]), weight[:LANES, :], 0, 0)
        att = att + mm(line_tokens(att_ref, source, where_ref[1]), weight[LANES:, :], 0, 0)
    for k, ref in ((0, outs[0]), (1, outs[1]), (3, outs[4])):
        ref[:ROWS, :] = att[ROWS * k : ROWS * (k + 1)].astype(BF)
        ref[ROWS:, :] = mix[ROWS * k : ROWS * (k + 1)].astype(BF)
    outs[2][...] = att[2 * ROWS : 3 * ROWS].astype(BF)
    outs[3][...] = mix[2 * ROWS : 3 * ROWS].astype(BF)


def out_projections(where, att, mix, weights):
    two, one = (2 * ROWS, WIDTH), (ROWS, WIDTH)
    shapes = (two, two, one, one, two)
    return pl.pallas_call(
        out_kernel,
        grid=(1,),
        in_specs=[pl.BlockSpec(memory_space=pltpu.SMEM)] + [once(*v.shape) for v in (att, mix, *weights)],
        out_specs=[once(*shape) for shape in shapes],
        out_shape=[jax.ShapeDtypeStruct(shape, BF) for shape in shapes],
        compiler_params=pltpu.CompilerParams(vmem_limit_bytes=VMEM_LIMIT),
        cost_estimate=pl.CostEstimate(
            flops=5_000_000_000, bytes_accessed=10_000_000, transcendentals=0
        ),
        name="out_projections",
    )(where, att, mix, *weights)


def out_back_kernel(where_ref, near, right, far_top, far_low, left, att_ref, mix_ref, w00, w01, w10, w11, *outs):
    d_att_ref, d_mix_ref, *grads = outs
    d_att = jnp.concatenate([near[:ROWS, :], right[:ROWS, :], far_top[...], left[:ROWS, :]], axis=0)
    d_mix = jnp.concatenate([near[ROWS:, :], right[ROWS:, :], far_low[...], left[ROWS:, :]], axis=0)
    x = where_ref[1]
    for a, b, weight, grad in (
        (0, 0, w00, grads[0]),
        (0, 1, w01, grads[1]),
        (1, 0, w10, grads[2]),
        (1, 1, w11, grads[3]),
    ):
        source = lax.rem(where_ref[0] + a, 2) * 2 + lax.rem(where_ref[2] + b, 2)
        d_mix_part = mm(weight[:LANES, :], d_mix, 1, 1).astype(BF)
        d_att_part = mm(weight[LANES:, :], d_att, 1, 1).astype(BF)
        for k in range(4):
            d_mix_ref[source, lax.rem(x + k, 4)] = d_mix_part[:, ROWS * k : ROWS * (k + 1)]
            d_att_ref[source, lax.rem(x + k, 4)] = d_att_part[:, ROWS * k : ROWS * (k + 1)]
        grad_mix = mm(line_tokens(mix_ref, source, x), d_mix)
        grad_att = mm(line_tokens(att_ref, source, x), d_att)
        together = jnp.concatenate([grad_mix, grad_att], axis=0).astype(BF)
        for i in range(8):
            grad[i] = together[OUT_BLOCK * i : OUT_BLOCK * (i + 1)]


def out_projections_back(where, d_proj, att, mix, weights):
    return pl.pallas_call(
        out_back_kernel,
        grid=(1,),
        in_specs=[pl.BlockSpec(memory_space=pltpu.SMEM)]
        + [once(*v.shape) for v in (*d_proj, att, mix, *weights)],
        out_specs=[once(4, 4, 128, ROWS), once(4, 4, LANES, ROWS)] + [once(8, OUT_BLOCK, WIDTH)] * 4,
        out_shape=[
            jax.ShapeDtypeStruct((4, 4, 128, ROWS), BF),
            jax.ShapeDtypeStruct((4, 4, LANES, ROWS), BF),
        ]
        + [jax.ShapeDtypeStruct((8, OUT_BLOCK, WIDTH), BF)] * 4,
        compiler_params=pltpu.CompilerParams(vmem_limit_bytes=VMEM_LIMIT),
        cost_estimate=pl.CostEstimate(
            flops=10_000_000_000, bytes_accessed=20_000_000, transcendentals=0
        ),
        name="out_projections_back",
    )(where, *d_proj, att, mix, *weights)


def halve_kernel(where_ref, kept_ref, came_ref, p0, p1, p2_top, p2_low, p3):
    for k, targets in ((0, (p0, p0)), (1, (p1, p1)), (2, (p2_top, p2_low)), (3, (p3, p3))):
        for h in range(2):
            spot = 4 * h + lax.rem(where_ref[1] + k, 4)
            total = (kept_ref[spot].astype(F32) + came_ref[spot].astype(F32)).astype(BF)
            if k == 2:
                targets[h][...] = total
            else:
                targets[h][ROWS * h : ROWS * (h + 1), :] = total


def halve(where, kept, came):
    two, one = (2 * ROWS, WIDTH), (ROWS, WIDTH)
    shapes = (two, two, one, one, two)
    return pl.pallas_call(
        halve_kernel,
        grid=(1,),
        in_specs=[pl.BlockSpec(memory_space=pltpu.SMEM), once(8, ROWS, WIDTH), once(8, ROWS, WIDTH)],
        out_specs=[once(*shape) for shape in shapes],
        out_shape=[jax.ShapeDtypeStruct(shape, BF) for shape in shapes],
        compiler_params=pltpu.CompilerParams(vmem_limit_bytes=VMEM_LIMIT),
        cost_estimate=pl.CostEstimate(flops=3_000_000, bytes_accessed=10_000_000, transcendentals=0),
        name="halve",
    )(where, kept, came)


def y_parts_kernel(yl_ref, near_0, came_0, near_1, came_1, p0, p1, p2_top, p2_low, p3):
    def total(half, at, count):
        near, came = ((near_0, came_0), (near_1, came_1))[half]
        rows = slice(at, at + count)
        return (near[rows].astype(F32) + came[rows].astype(F32)).astype(BF)

    for yl in range(2):

        @pl.when(yl_ref[0] == yl)
        def _():
            p0[...] = total(0, 4 * yl, 4)
            p1[...] = total(yl, 4 * (1 - yl), 4)
            p2_top[...] = total(1, 4 * yl, 2)
            p2_low[...] = total(1, 4 * yl + 2, 2)
            p3[...] = total(1 - yl, 4 * (1 - yl), 4)


def y_parts(yl, near_0, came_0, near_1, came_1):
    block = near_0.shape[1:]
    shapes = [(count,) + block for count in (4, 4, 2, 2, 4)]
    return pl.pallas_call(
        y_parts_kernel,
        grid=(1,),
        in_specs=[pl.BlockSpec(memory_space=pltpu.SMEM)] + [once(*near_0.shape)] * 4,
        out_specs=[once(*shape) for shape in shapes],
        out_shape=[jax.ShapeDtypeStruct(shape, BF) for shape in shapes],
        compiler_params=pltpu.CompilerParams(vmem_limit_bytes=VMEM_LIMIT),
        cost_estimate=pl.CostEstimate(flops=4_000_000, bytes_accessed=20_000_000, transcendentals=0),
        name="y_parts",
    )(yl, near_0, came_0, near_1, came_1)


def z_parts_kernel(z_ref, *refs):
    ff, out, parts = refs[:3], refs[3:6], refs[6:]

    def total(terms, k):
        at = lax.rem(z_ref[0] + k, 4)
        return sum(term[at].astype(F32) for term in terms)

    for k in range(4):
        empty = jnp.zeros((RING_ROWS - FF_BLOCK - OUT_BLOCK, WIDTH), F32)
        block = jnp.concatenate([total(out, k), total(ff, k), empty], axis=0).astype(BF)
        if k == 2:
            parts[2][...] = block[: RING_ROWS // 2]
            parts[3][...] = block[RING_ROWS // 2 :]
        else:
            parts[(0, 1, 2, 4)[k]][...] = block


def z_parts(z, ff, out):
    one, half = (RING_ROWS, WIDTH), (RING_ROWS // 2, WIDTH)
    shapes = (one, one, half, half, one)
    return pl.pallas_call(
        z_parts_kernel,
        grid=(1,),
        in_specs=[pl.BlockSpec(memory_space=pltpu.SMEM)] + [once(*v.shape) for v in (*ff, *out)],
        out_specs=[once(*shape) for shape in shapes],
        out_shape=[jax.ShapeDtypeStruct(shape, BF) for shape in shapes],
        compiler_params=pltpu.CompilerParams(vmem_limit_bytes=VMEM_LIMIT),
        cost_estimate=pl.CostEstimate(flops=4_000_000, bytes_accessed=10_000_000, transcendentals=0),
        name="z_parts",
    )(z, *ff, *out)


def one_hot(rows, columns, offset, limit=None):
    row = lax.broadcasted_iota(jnp.int32, (rows, columns), 0)
    column = lax.broadcasted_iota(jnp.int32, (rows, columns), 1)
    hit = column == row + offset
    if limit is not None:
        hit = hit & (row < limit)
    return hit.astype(F32).astype(BF)


def head_places(me):
    filled = jnp.where(me == 15, 0, jnp.where(lax.rem(me, 3) == 2, HEAD, 2 * HEAD))
    return 20 * lax.div(me, 3) + 28 * lax.rem(me, 3), filled, 200 - 8 * me


def to_heads_kernel(me_ref, att_0, att_1, att_2, mix_before, mix_own, extra_0, extra_1, out_ref):
    att_at, filled, mix_at = head_places(me_ref[0])
    mix = mm(one_hot(192, 200, mix_at), mix_before[...]) + mm(one_hot(192, 200, mix_at - 200), mix_own[...])
    att = jnp.zeros((128, WIDTH), F32)
    for t, rows in enumerate((att_0, att_1, att_2)):
        att = att + mm(one_hot(128, 100, att_at - 100 * t, filled), rows[...])
    out_ref[:192, :] = mix.astype(BF)
    out_ref[192:256, :] = extra_0[...] + extra_1[...]
    out_ref[256:, :] = att.astype(BF)


def to_heads(me, rows):
    return pl.pallas_call(
        to_heads_kernel,
        grid=(1,),
        in_specs=[pl.BlockSpec(memory_space=pltpu.SMEM)] + [once(*v.shape) for v in rows],
        out_specs=once(384, WIDTH),
        out_shape=jax.ShapeDtypeStruct((384, WIDTH), BF),
        compiler_params=pltpu.CompilerParams(vmem_limit_bytes=VMEM_LIMIT),
        cost_estimate=pl.CostEstimate(flops=600_000_000, bytes_accessed=4_000_000, transcendentals=0),
        name="to_heads",
    )(me, *rows)


def finish_kernel(me_ref, z_ref, *refs):
    pieces, refs = refs[:5], refs[5:]
    gateup_ref, down_ref, att_0, att_1, att_2, mix_before, mix_own, extra_ref, blocks_ref, out_ref = refs
    for spot, block in rep_spots(z_ref, pieces):
        blocks_ref[spot] = block
    for half in range(2):
        for z in range(4):
            block = blocks_ref[2 * z + half].astype(F32)
            i = 4 * half + z
            out_ref[OUT_BLOCK * i : OUT_BLOCK * (i + 1), :] = block[:OUT_BLOCK].astype(BF)
            start, stop = FF_BLOCK * i, min(FF_BLOCK * (i + 1), 3 * FF_ROWS)
            rows = block[OUT_BLOCK : OUT_BLOCK + FF_BLOCK]
            edge = 2 * FF_ROWS
            if start < edge:
                end = min(stop, edge)
                gateup_ref[start:end, :] = rows[: end - start]
            if stop > edge:
                begin = max(start, edge)
                down_ref[begin - edge : stop - edge, :] = rows[begin - start : stop - start]
    att_at, filled, mix_at = head_places(me_ref[0])
    mix, att = out_ref[:192, :], out_ref[256:, :]
    for t, target in enumerate((att_0, att_1, att_2)):
        kept = mm(one_hot(128, 100, att_at - 100 * t, filled), att, 0, 0)
        target[...] = kept.astype(BF)
    mix_before[...] = mm(one_hot(192, 200, mix_at), mix, 0, 0).astype(BF)
    mix_own[...] = mm(one_hot(192, 200, mix_at - 200), mix, 0, 0).astype(BF)
    extra_ref[...] = out_ref[192:256, :]


def finish(me, z, pieces):
    shapes = (
        [((2 * FF_ROWS, WIDTH), F32), ((FF_ROWS, WIDTH), F32)]
        + [((100, WIDTH), BF)] * 3
        + [((200, WIDTH), BF)] * 2
        + [((64, WIDTH), BF)]
    )
    return pl.pallas_call(
        finish_kernel,
        grid=(1,),
        in_specs=[pl.BlockSpec(memory_space=pltpu.SMEM)] * 2 + [once(*v.shape) for v in pieces],
        out_specs=[once(*shape) for shape, _ in shapes],
        out_shape=[jax.ShapeDtypeStruct(shape, kind) for shape, kind in shapes],
        scratch_shapes=[
            pltpu.VMEM((8, RING_ROWS, WIDTH), BF),
            pltpu.VMEM((8 * OUT_BLOCK, WIDTH), BF),
        ],
        compiler_params=pltpu.CompilerParams(vmem_limit_bytes=VMEM_LIMIT),
        cost_estimate=pl.CostEstimate(flops=600_000_000, bytes_accessed=16_000_000, transcendentals=0),
        name="finish",
    )(me, z, *pieces)


def root_norm(values, gain):
    return values * lax.rsqrt(jnp.mean(values * values, axis=-1, keepdims=True) + 1e-06) * gain


def branch_sum(attend_proj, mixer_proj, attend_gain, mixer_gain):
    return root_norm(attend_proj, attend_gain) + root_norm(mixer_proj, mixer_gain)


Y = ("yl", "yh")
SIZES = {"x": 4, "z": 4, "core": 2, "yh": 2, "yl": 2, SHARD: PEERS, Y: 4}


def shift(v, axis, by):
    n, shape = SIZES[axis], v.shape
    if shape[-2] % 16 == 0:
        v = v.reshape(shape[:-2] + (shape[-2] // 16, 16, shape[-1]))
    order = (0, 2, 1, 3) if axis == Y else range(n)
    pairs = [(order[i], order[(i + by) % n]) for i in range(n)]
    return lax.ppermute(v, axis, pairs).reshape(shape)


def gather_x(v, cut=64):
    left = shift(v, "x", 1)
    right = shift(v, "x", -1)
    return [v, right, shift(left[:cut], "x", 1), shift(right[cut:], "x", -1), left]


def add_low(a, b):
    return (a.astype(F32) + b.astype(F32)).astype(BF)


def ring_first(parts, axis):
    p0, p1, top, low, p3 = parts
    cut = top.shape[0]
    top = shift(top, axis, 1)
    low = shift(low, axis, -1)
    ahead = jnp.concatenate([add_low(p1[:cut], top), p1[cut:]], axis=0)
    behind = jnp.concatenate([p3[:cut], add_low(p3[cut:], low)], axis=0)
    return p0, ahead, behind


def ring_second(p0, ahead, behind, axis):
    return p0, shift(ahead, axis, 1), shift(behind, axis, -1)


def total(terms):
    return sum(term.astype(F32) for term in terms)


def reduce_x(parts):
    return total(ring_second(*ring_first(parts, "x"), "x"))


def spread_sum(blocks, axes):
    came = lax.all_to_all(blocks, axes, 0, 0, tiled=False)
    return jnp.sum(came.astype(F32), axis=0).astype(BF)


def rep_gather(v):
    return lax.all_to_all(jnp.broadcast_to(v[None], (8,) + v.shape), REP, 0, 0, tiled=False)


def collect_states(w):
    n = w.shape[0]
    return jnp.concatenate([w[:, :, :3].reshape(n, 48), w[:, :2, 3]], axis=1)


def local(
    tokens,
    segments,
    input_gain,
    attention_weight,
    attend_out,
    mixer_weight,
    param_weight,
    mixer_out,
    attend_gain,
    mixer_gain,
    feed_gain,
    gateup_weight,
    down_weight,
    decay_log,
    step_bias,
    skip_gain,
    cotangent,
):
    me = lax.axis_index(SHARD)
    yh, x, core = lax.axis_index("yh"), lax.axis_index("x"), lax.axis_index("core")
    where = jnp.stack([yh, x, core]).astype(jnp.int32)
    core_word = where[2:]
    me_word = me.astype(jnp.int32)[None]
    yl_word, z_word = (lax.axis_index(name).astype(jnp.int32)[None] for name in ("yl", "z"))
    grouped = (ROWS // 16, 16, WIDTH)
    tok_low, grad_out = tokens.reshape(grouped), cotangent.reshape(grouped)
    tok = tok_low.astype(F32)
    tok_low, grad_out = tok_low.reshape(ROWS, WIDTH), grad_out.reshape(ROWS, WIDTH)

    gains = jnp.concatenate([input_gain, attend_gain, mixer_gain, feed_gain])
    extra = jnp.concatenate(
        [
            jnp.pad(segments.astype(BF), ((0, 0), (0, WIDTH - ROWS))),
            jnp.pad(gains[None], ((0, 0), (0, WIDTH - 400))),
            jnp.zeros((14, WIDTH), BF),
        ],
        axis=0,
    )
    block = jnp.concatenate([tok_low, extra], axis=0)
    far_block = shift(block, "yh", 1)
    left, right = shift(block, "x", 1), shift(block, "x", -1)
    far_block, left, right, attention_weight, mixer_weight, param_weight = lax.optimization_barrier(
        (far_block, left, right, attention_weight, mixer_weight, param_weight)
    )
    far_left, far_right = shift(far_block, "x", 1), shift(far_block, "x", -1)
    blocks = [block, right, shift(left[:64], "x", 1), shift(right[64:], "x", -1), left]
    spread = spread_inputs(attention_weight, mixer_weight, param_weight)
    spread, far_left, far_right, blocks = lax.optimization_barrier((spread, far_left, far_right, blocks))
    blocks += [far_block, far_right, shift(far_left[:64], "x", 1), shift(far_right[64:], "x", -1), far_left]
    weight_in = lax.all_to_all(spread, SHARD, 0, 0, tiled=False).reshape(WIDTH, IN_WIDTH)
    mine = place(where, blocks)
    other = shift(mine, "core", 1)
    low_rows = jnp.stack(in_order(core, mine[:, ROWS : ROWS + 2, :400], other[:, ROWS : ROWS + 2, :400]), axis=1)
    seg = low_rows[:, :, 0, :ROWS].reshape(LENGTH).astype(jnp.int32)
    all_gains = low_rows[:, :, 1].reshape(PEERS, 4, 100).transpose(1, 0, 2)
    gain_in, gain_attend, gain_mixer, gain_feed = all_gains.reshape(4, WIDTH).astype(F32)

    own_attout, own_mixout, _ = lax.optimization_barrier((attend_out, mixer_out, mine))
    own_heads = to_heads(
        me_word,
        (
            own_attout,
            shift(own_attout, SHARD, -1),
            shift(own_attout, SHARD, -2),
            shift(own_mixout, SHARD, 1),
            own_mixout,
            lax.ppermute(own_mixout[72:136], SHARD, [(15, 0)]),
            lax.ppermute(own_mixout[136:200], SHARD, [(15, 1)]),
        ),
    )
    own_heads, weight_in = lax.optimization_barrier((own_heads, weight_in))
    far_heads = shift(own_heads, "yh", 1)
    own_down, own_gateup, _ = lax.optimization_barrier(
        (down_weight, gateup_weight.transpose(1, 2, 0).reshape(2 * FF_ROWS, WIDTH), own_heads)
    )
    far_down, far_gateup = shift(own_down, "yh", 1), shift(own_gateup, "yh", 1)
    normed, projected, kv, kvt = project(core_word, mine, other, gain_in[None], weight_in)
    seg_col, seg_row = seg[:, None], seg[None]
    attended, logs = attend(projected, kv, kvt, seg_col, seg_row)
    attended = lax.all_to_all(attended.reshape(4, 4, 128, ROWS), ("yh", "core"), 0, 0, tiled=False)
    late_grad_out, logs, states_projected = lax.optimization_barrier((grad_out, logs, projected))
    some_grad_out = gather_x(late_grad_out)

    slot_heads = jnp.concatenate([3 * me + jnp.arange(3), jnp.minimum(48 + me, 49)[None]])
    valid = jnp.concatenate([jnp.ones((3,), F32), (me < 2).astype(F32)[None]])
    chunk_segs = seg.reshape(LENGTH // CHUNK, CHUNK)
    last = chunk_segs[:, -1]
    before = jnp.concatenate([last[:1] * 0 - 1, last[:-1]])
    flags = jnp.stack(
        [(chunk_segs == before[:, None]).reshape(-1), (chunk_segs == last[:, None]).reshape(-1)], axis=1
    ).astype(F32)
    par = jnp.pad(jnp.stack([-jnp.exp(decay_log[slot_heads]), step_bias[slot_heads]]), ((0, 0), (0, 4)))
    skip = jnp.repeat(skip_gain[slot_heads], 64)[None]
    state_args = (states_projected, flags, seg_col, seg_row, par, skip)
    mixed, states_y, entries = states(*state_args)
    mixed, attended = lax.optimization_barrier((mixed, attended))
    mixed = lax.all_to_all(mixed.reshape(4, 4, LANES, ROWS), ("yh", "core"), 0, 0, tiled=False)

    mixed, far_heads, far_down, far_gateup = lax.optimization_barrier((mixed, far_heads, far_down, far_gateup))
    out_weights = [own_heads, shift(own_heads, "core", 1), far_heads, shift(far_heads, "core", 1)]
    downs = [own_down, shift(own_down, "core", 1), far_down, shift(far_down, "core", 1)]
    gateups = [own_gateup, shift(own_gateup, "core", 1), far_gateup, shift(far_gateup, "core", 1)]
    both = reduce_x(out_projections(where, attended, mixed, out_weights)).reshape(2, *grouped)
    attend_proj, mixer_proj = both[0], both[1]
    middle = tok + branch_sum(attend_proj, mixer_proj, gain_attend, gain_mixer)
    feed_in = root_norm(middle, gain_feed).astype(BF).reshape(ROWS, WIDTH)

    fed = feed_forward(gather_x(feed_in), some_grad_out, gateups, downs)
    some_feed, some_grad, hidden, d_gate_up = fed[:4]
    out_parts, d_feed_parts = fed[4:9], fed[9:]
    p0, ahead, behind = ring_first(d_feed_parts, "x")
    near_1, far_1 = feed_grads(1, some_feed, some_grad, hidden, d_gate_up)
    ahead, behind, far_1 = lax.optimization_barrier((ahead, behind, far_1))
    d_feed_in = total(ring_second(p0, ahead, behind, "x")).reshape(grouped)
    far_1 = shift(far_1, "core", 1)

    _, feed_pull = jax.vjp(root_norm, middle, gain_feed)
    middle_part, g_feed = feed_pull(d_feed_in)
    d_middle = grad_out.reshape(grouped).astype(F32) + middle_part
    _, branch_pull = jax.vjp(branch_sum, attend_proj, mixer_proj, gain_attend, gain_mixer)
    d_attproj, d_mixproj, g_attend, g_mixer = branch_pull(d_middle)
    d_both = jnp.stack([d_attproj, d_mixproj]).astype(BF).reshape(2 * ROWS, WIDTH)
    left, right = shift(d_both, "x", 1), shift(d_both, "x", -1)
    near_0, far_0 = feed_grads(0, some_feed, some_grad, hidden, d_gate_up)
    left, right, far_0 = lax.optimization_barrier((left, right, far_0))
    d_proj = [d_both, right, shift(left[:ROWS], "x", 1), shift(right[ROWS:], "x", -1), left]
    far_0 = shift(far_0, "core", 1)
    ff_parts = y_parts(yl_word, near_0, far_0, near_1, far_1)
    out_first_x = ring_first(out_parts, "x")
    d_proj, ff_parts, out_first_x = lax.optimization_barrier((d_proj, ff_parts, out_first_x))
    ff_first = ring_first(ff_parts, Y)
    d_attended, d_mixed, out_00, out_01, out_10, out_11 = out_projections_back(
        where, d_proj, attended, mixed, out_weights
    )
    d_mixed = lax.all_to_all(d_mixed, ("yh", "core"), 0, 0, tiled=False).reshape(2, 2, 4, LANES, ROWS)
    d_attended = lax.all_to_all(d_attended, ("yh", "core"), 0, 0, tiled=False).reshape(2, 2, 4, 128, ROWS)

    out_ring = y_parts(yl_word, out_00, shift(out_01, "core", 1), out_10, shift(out_11, "core", 1))

    out_terms_x = ring_second(*out_first_x, "x")
    d_mixed, out_ring, ff_first, out_terms_x = lax.optimization_barrier(
        (d_mixed, out_ring, ff_first, out_terms_x)
    )
    result = (middle + total(out_terms_x).reshape(grouped)).astype(BF)
    ff_terms = ring_second(*ff_first, Y)
    out_first = ring_first(out_ring, Y)
    d_x, d_z, d_bcr, d_par, d_skip = states_back(*state_args, states_y, entries, d_mixed)
    d_x, ff_terms, out_first = lax.optimization_barrier((d_x, ff_terms, out_first))
    heads = jnp.stack([d_par[0, :SLOTS], d_par[1, :SLOTS], d_skip.reshape(SLOTS, 64).sum(axis=1)]) * valid
    heads = jnp.broadcast_to(heads.reshape(1, 3 * SLOTS), (PEERS, 3 * SLOTS))
    small = jnp.concatenate(
        [jnp.pad(g.reshape(PEERS, -1), ((0, 0), (0, 128 - g.size // PEERS))) for g in (g_attend, g_mixer, g_feed, heads)]
        + [jnp.zeros((PEERS, 128), F32)],
        axis=1,
    )
    in_states = in_grads(normed, (d_x, d_z, d_bcr), weight_in[:, 256:], small)
    out_terms = ring_second(*out_first, Y)
    d_attended, in_states, out_terms = lax.optimization_barrier((d_attended, in_states, out_terms))
    in_states = lax.all_to_all(in_states, SHARD, 0, 0, tiled=False)
    first = ring_first(z_parts(z_word, ff_terms, out_terms), "z")
    d_q, d_kv = attend_back(projected, d_attended, kv, kvt, seg_col, seg_row, logs)
    d_q, d_kv, in_states, first = lax.optimization_barrier((d_q, d_kv, in_states, first))
    in_states = spread_sum(in_states.reshape(8, 2, 104, 640), REP)
    terms = ring_second(*first, "z")
    in_heads = in_grads(normed, (d_q, d_kv), weight_in[:, :256], jnp.zeros((PEERS, 256), F32))
    in_states, in_heads, d_q, terms = lax.optimization_barrier((in_states, in_heads, d_q, terms))
    in_heads = lax.all_to_all(in_heads, SHARD, 0, 0, tiled=False)
    yl = yl_word[0]
    rep_block = total(terms).astype(BF)
    pair = jnp.stack(in_order(yl, rep_block, shift(rep_block, "yl", 1)))
    states_pair = jnp.stack(in_order(yl, in_states, shift(in_states, "yl", 1)))

    kept, sent = d_normed_parts(core_word, (d_q, d_kv, d_x, d_z, d_bcr), weight_in)
    line_parts = halve(where, kept, shift(sent, "core", 1))
    in_heads, line_parts, pair, states_pair = lax.optimization_barrier((in_heads, line_parts, pair, states_pair))
    in_heads = spread_sum(in_heads.reshape(8, 2, 104, 256), REP)
    line_first = ring_first(line_parts, "x")
    left, right = shift(pair, "z", 1), shift(pair, "z", -1)
    states_left, states_right = shift(states_pair, "z", 1), shift(states_pair, "z", -1)
    in_heads, line_first, left, right, states_left, states_right = lax.optimization_barrier(
        (in_heads, line_first, left, right, states_left, states_right)
    )
    in_heads = rep_gather(in_heads).reshape(PEERS, 104, 256)
    line_terms = ring_second(*line_first, "x")
    pieces = [pair, right, shift(left[0], "z", 1), shift(right[1], "z", -1), left]
    states_pieces = [
        states_pair,
        states_right,
        shift(states_left[0], "z", 1),
        shift(states_right[1], "z", -1),
        states_left,
    ]
    line_terms, pieces = lax.optimization_barrier((line_terms, pieces))
    sum_gateup, sum_down, *out_rows = finish(me_word, z_word, pieces)
    in_heads, line_terms, out_rows, states_pieces = lax.optimization_barrier(
        (in_heads, line_terms, out_rows, states_pieces)
    )
    att_0, att_1, att_2, mix_before, mix_own, extra = out_rows
    line = total(line_terms)
    line_kept, line_sent = in_order(yh, line[:ROWS], line[ROWS:])
    d_normed = (line_kept + shift(line_sent.astype(BF), "yh", 1)).reshape(grouped)
    _, input_pull = jax.vjp(lambda t: root_norm(t, gain_in), tok)
    grad_tokens = (d_middle + input_pull(d_normed)[0]).astype(BF)

    sum_attention, sum_mixer, sum_param, low_states, low_heads = collect(z_word, states_pieces, in_heads)
    totals = jnp.sum(low_states, axis=0)
    own_in = (totals[512:612] + jnp.sum(low_heads, axis=0)[128:228]) / input_gain.astype(F32)
    g_decay, g_bias, g_skip = collect_states(
        low_states[:, 384 : 384 + 3 * SLOTS].reshape(PEERS, 3, SLOTS).transpose(1, 0, 2)
    )
    sum_gateup = sum_gateup.reshape(2, FF_ROWS, WIDTH).transpose(2, 0, 1)
    sum_attout = total([att_0, shift(att_1, SHARD, 1), shift(att_2, SHARD, 2)])
    extra_0 = jnp.pad(lax.ppermute(extra, SHARD, [(0, 15)]), ((72, 64), (0, 0)))
    extra_1 = jnp.pad(lax.ppermute(extra, SHARD, [(1, 15)]), ((136, 0), (0, 0)))
    sum_mixout = total([mix_own, shift(mix_before, SHARD, -1), extra_0, extra_1])
    return (
        result.reshape(1, ROWS, WIDTH),
        grad_tokens.reshape(1, ROWS, WIDTH),
        own_in,
        sum_attention,
        sum_attout,
        sum_mixer,
        sum_param,
        sum_mixout,
        totals[:100],
        totals[128:228],
        totals[256:356],
        sum_gateup,
        sum_down,
        g_decay,
        g_bias,
        g_skip,
    )


def solution(mesh):
    fine = Mesh(mesh.devices.reshape(4, 2, 2, 4, 2), ("z", "yl", "yh", "x", "core"))
    rows = P(REP, SHARD, None)
    matrix = P(SHARD, None)
    vector = P(SHARD)
    return jax.shard_map(
        local,
        mesh=fine,
        in_specs=(
            rows,
            P(REP, SHARD),
            vector,
            matrix,
            matrix,
            matrix,
            matrix,
            matrix,
            vector,
            vector,
            vector,
            P(None, None, SHARD),
            matrix,
            P(),
            P(),
            P(),
            rows,
        ),
        out_specs=(
            rows,
            rows,
            vector,
            matrix,
            matrix,
            matrix,
            matrix,
            matrix,
            vector,
            vector,
            vector,
            P(None, None, SHARD),
            matrix,
            P(),
            P(),
            P(),
        ),
        check_vma=False,
    )
```

```python
import jax
import jax.numpy as jnp
from jax import lax
from jax.experimental import pallas as pl
from jax.experimental.pallas import tpu as pltpu
from jax.sharding import Mesh
from jax.sharding import PartitionSpec as P

QUERY_HEADS = 25
HEAD = 64
KV_HEADS = 5
GROUP = 5
WINDOW = 1024
SH = 50
NS = 16
DI = 3200
WIDTH = 1600
FF_ROWS = 344
FF_BLOCK = 136
OUT_BLOCK = 48
RING_ROWS = 192
VMEM_LIMIT = 57 * 1024 * 1024
LENGTH = 2048
PEERS = 16
ROWS = 128
SLOTS = 4
CHUNK = 128
REP = ("z", "yl")
SHARD = ("yh", "x", "core")
SCALE = HEAD**-0.5
IN_WIDTH = 896
BF = jnp.bfloat16
F32 = jnp.float32
HI = lax.Precision.HIGHEST


def mm(a, b, ca=1, cb=0):
    return lax.dot_general(
        a.astype(BF), b.astype(BF), (((ca,), (cb,)), ((), ())), preferred_element_type=F32
    )


def mm32(a, b, ca=1, cb=0):
    return lax.dot_general(
        a, b, (((ca,), (cb,)), ((), ())), precision=HI, preferred_element_type=F32
    )


QB = 256
PARTS = WINDOW // QB + 1
SPAN = QB * PARTS
BLOCKS = LENGTH // QB


def key_parts(step):
    blocks = [step - (PARTS - 1) + j for j in range(PARTS)]
    starts = [pl.multiple_of(jnp.maximum(block, 0) * QB, QB) for block in blocks]
    return starts, [jnp.where(block < 0, 1024, 0) for block in blocks]


def allowed_parts(key_segs, query_segs, starts, missing):
    key = lax.broadcasted_iota(jnp.int32, (QB, QB), 0)
    query = lax.broadcasted_iota(jnp.int32, (QB, QB), 1)
    masks = []
    for j in range(PARTS):
        mask = key_segs[pl.ds(starts[j], QB), :] + missing[j] == query_segs
        if j == 0:
            mask = mask & (key > query)
        if j == PARTS - 1:
            mask = mask & (key <= query)
        masks.append(mask)
    return masks


def scaled(q):
    return (q.astype(BF).astype(F32) * SCALE).astype(BF)


def attend_kernel(q_ref, kv_ref, kvt_ref, key_segs, query_segs, out_ref, log_ref):
    starts, missing = key_parts(pl.program_id(0))
    masks = allowed_parts(key_segs, query_segs[...], starts, missing)
    for h in range(2):
        q = scaled(q_ref[:, HEAD * h : HEAD * (h + 1)])
        scores = []
        for j in range(PARTS):
            s = mm(kv_ref[pl.ds(starts[j], QB), :HEAD], q, 1, 1)
            scores.append(jnp.where(masks[j], s, -1e30))
        top = scores[0]
        for s in scores[1:]:
            top = jnp.maximum(top, s)
        top = jnp.max(top, axis=0, keepdims=True)
        shifted = [jnp.exp(s - top) for s in scores]
        total = shifted[0]
        for s in shifted[1:]:
            total = total + s
        total = jnp.sum(total, axis=0, keepdims=True)
        inverse = 1.0 / total
        out = jnp.zeros((HEAD, QB), F32)
        for j in range(PARTS):
            soft = (shifted[j] * inverse).astype(BF)
            out = out + mm(kvt_ref[HEAD:, pl.ds(starts[j], QB)], soft)
        for c in range(2):
            out_ref[0, c, 0, HEAD * h : HEAD * (h + 1), :] = out[:, ROWS * c : ROWS * (c + 1)].astype(BF)
        log_ref[h : h + 1, :] = top + jnp.log(total)


def attend_back_kernel(
    q_ref, g_ref, kv_ref, kvt_ref, key_segs, query_segs, log_ref, dq_ref, dkv_ref, dk_acc, dv_acc
):
    step = pl.program_id(0)
    starts, missing = key_parts(step)

    @pl.when(step == 0)
    def _():
        dk_acc[...] = jnp.zeros_like(dk_acc)
        dv_acc[...] = jnp.zeros_like(dv_acc)

    masks = allowed_parts(key_segs, query_segs[...], starts, missing)
    g_t = jnp.concatenate([g_ref[0, 0, 0], g_ref[0, 1, 0]], axis=1)
    g_all = g_t.astype(F32).T.astype(BF)
    dqs = []
    for h in range(2):
        q = scaled(q_ref[:, HEAD * h : HEAD * (h + 1)])
        g = g_all[:, HEAD * h : HEAD * (h + 1)]
        log_total = log_ref[h : h + 1, :]
        softs, grads = [], []
        delta = jnp.zeros((QB, QB), F32)
        for j in range(PARTS):
            rows = pl.ds(starts[j], QB)
            s = mm(kv_ref[rows, :HEAD], q, 1, 1)
            soft = jnp.exp(jnp.where(masks[j], s - log_total, -1e30))
            d_soft = mm(kv_ref[rows, HEAD:], g_t[HEAD * h : HEAD * (h + 1), :])
            delta = delta + soft * d_soft
            dv_acc[rows, :] += mm(soft, g)
            softs.append(soft)
            grads.append(d_soft)
        delta = jnp.sum(delta, axis=0, keepdims=True)
        dq = jnp.zeros((HEAD, QB), F32)
        for j in range(PARTS):
            rows = pl.ds(starts[j], QB)
            d_scores = (softs[j] * (grads[j] - delta)).astype(BF)
            dk_acc[rows, :] += mm(d_scores, q)
            dq = dq + mm(kvt_ref[:HEAD, rows], d_scores)
        dqs.append(dq * SCALE)
    dq_ref[...] = jnp.concatenate(dqs, axis=0).T.astype(BF)

    @pl.when(step == BLOCKS - 1)
    def _():
        dkv_ref[...] = jnp.concatenate([dk_acc[...], dv_acc[...]], axis=1).astype(BF)


def whole(*shape):
    return pl.BlockSpec(shape, lambda i: (0,) * len(shape))


def attend(projected, kv, kvt, key_segs, query_segs):
    return pl.pallas_call(
        attend_kernel,
        grid=(BLOCKS,),
        in_specs=[
            pl.BlockSpec((QB, 128), lambda i: (i, 0)),
            whole(LENGTH, 128),
            whole(128, LENGTH),
            whole(LENGTH, 1),
            pl.BlockSpec((1, QB), lambda i: (0, i)),
        ],
        out_specs=[
            pl.BlockSpec((1, 2, 1, 128, ROWS), lambda i: (i // 4, 0, i % 4, 0, 0)),
            pl.BlockSpec((8, QB), lambda i: (0, i)),
        ],
        out_shape=[
            jax.ShapeDtypeStruct((2, 2, 4, 128, ROWS), BF),
            jax.ShapeDtypeStruct((8, LENGTH), F32),
        ],
        compiler_params=pltpu.CompilerParams(vmem_limit_bytes=VMEM_LIMIT),
        cost_estimate=pl.CostEstimate(
            flops=10_000_000_000, bytes_accessed=4_000_000, transcendentals=5_300_000
        ),
        name="attend",
    )(projected, kv, kvt, key_segs, query_segs)


def attend_back(projected, g, kv, kvt, key_segs, query_segs, logs):
    return pl.pallas_call(
        attend_back_kernel,
        grid=(BLOCKS,),
        in_specs=[
            pl.BlockSpec((QB, 128), lambda i: (i, 0)),
            pl.BlockSpec((1, 2, 1, 128, ROWS), lambda i: (i // 4, 0, i % 4, 0, 0)),
            whole(LENGTH, 128),
            whole(128, LENGTH),
            whole(LENGTH, 1),
            pl.BlockSpec((1, QB), lambda i: (0, i)),
            pl.BlockSpec((8, QB), lambda i: (0, i)),
        ],
        out_specs=[
            pl.BlockSpec((QB, 128), lambda i: (i, 0)),
            whole(LENGTH, 128),
        ],
        out_shape=[
            jax.ShapeDtypeStruct((LENGTH, 128), BF),
            jax.ShapeDtypeStruct((LENGTH, 128), BF),
        ],
        scratch_shapes=[
            pltpu.VMEM((LENGTH, HEAD), F32),
            pltpu.VMEM((LENGTH, HEAD), F32),
        ],
        compiler_params=pltpu.CompilerParams(vmem_limit_bytes=VMEM_LIMIT),
        cost_estimate=pl.CostEstimate(
            flops=25_000_000_000, bytes_accessed=5_000_000, transcendentals=5_300_000
        ),
        name="attend_back",
    )(projected, g, kv, kvt, key_segs, query_segs, logs)


LANES = SLOTS * 64
CHUNKS = LENGTH // CHUNK
PAIR = 2
STEP = PAIR * CHUNK
STEPS = LENGTH // STEP


def head_selector(transposed=False):
    shape = (LANES, 8) if transposed else (8, LANES)
    head = lax.broadcasted_iota(jnp.int32, shape, 1 if transposed else 0)
    lane = lax.broadcasted_iota(jnp.int32, shape, 0 if transposed else 1)
    return (lane // 64 == head).astype(F32)


def softplus(v):
    return jnp.maximum(v, 0.0) + jnp.log1p(jnp.exp(-jnp.abs(v)))


def chunk_values(u, x_ref, bcr_ref, flags_ref, seg_col, seg_row, par_ref):
    rows = slice(CHUNK * u, CHUNK * (u + 1))
    row = lax.broadcasted_iota(jnp.int32, (CHUNK, CHUNK), 0)
    col = lax.broadcasted_iota(jnp.int32, (CHUNK, CHUNK), 1)
    linked = (row >= col) & (seg_col[rows, :] == seg_row[:, rows])
    b, c = bcr_ref[rows, :NS], bcr_ref[rows, NS : 2 * NS]
    raw = bcr_ref[rows, 2 * NS : 2 * NS + 8] + par_ref[1:2, :]
    step = softplus(raw)
    logs = step * par_ref[0:1, :]
    cum = mm32((row >= col).astype(F32), logs)
    carry = flags_ref[rows, 0:1] * jnp.exp(cum)
    tail = flags_ref[rows, 1:2] * jnp.exp(cum[CHUNK - 1 : CHUNK, :] - cum)
    wide = mm32(jnp.concatenate([step, carry, tail], axis=0), head_selector())
    step_w, carry_w, tail_w = wide[:CHUNK], wide[CHUNK : 2 * CHUNK], wide[2 * CHUNK :]
    cum_t = cum.T
    inner = mm32(c, b, 1, 1)
    decays = []
    for h in range(SLOTS):
        gap = jnp.minimum(cum[:, h : h + 1] - cum_t[h : h + 1, :], 0.0)
        decays.append(jnp.where(linked, jnp.exp(gap), 0.0))
    drive = step_w * x_ref[rows, :]
    return b, c, raw, step, logs, step_w, carry_w, tail_w, inner, decays, drive


def by_head(values):
    selector = head_selector()
    return [(values * selector[h : h + 1, :]).astype(BF) for h in range(SLOTS)]


def state_kernel(
    x_ref, z_ref, bcr_ref, flags_ref, seg_col, seg_row, par_ref, skip_ref, mixed_ref, y_ref, entry_ref, state
):
    @pl.when(pl.program_id(0) == 0)
    def _():
        state[...] = jnp.zeros_like(state)

    entry = state[...]
    for u in range(PAIR):
        rows = slice(CHUNK * u, CHUNK * (u + 1))
        b, c, _, _, _, _, carry_w, tail_w, inner, decays, drive = chunk_values(
            u, x_ref, bcr_ref, flags_ref, seg_col, seg_row, par_ref
        )
        kernels = jnp.concatenate([(d * inner).astype(BF) for d in decays], axis=1)
        drives = jnp.concatenate(by_head(drive), axis=0)
        y = mm(kernels, drives) + skip_ref[...] * x_ref[rows, :]
        ends = mm(b, tail_w * drive, 0, 0)
        entry_ref[u] = entry
        y = y + carry_w * mm(c, entry)
        entry = carry_w[CHUNK - 1 : CHUNK, :] * entry + ends
        y_ref[rows, :] = y
        z = z_ref[rows, :]
        mixed_ref[0, u, 0] = (y * z * jax.nn.sigmoid(z)).T.astype(BF)
    state[...] = entry


def state_back_kernel(
    x_ref,
    z_ref,
    bcr_ref,
    flags_ref,
    seg_col,
    seg_row,
    par_ref,
    skip_ref,
    y_ref,
    entry_ref,
    g_ref,
    dx_ref,
    dz_ref,
    dbcr_ref,
    dpar_ref,
    dskip_ref,
    d_state,
):
    @pl.when(pl.program_id(0) == 0)
    def _():
        d_state[...] = jnp.zeros_like(d_state)
        dpar_ref[...] = jnp.zeros_like(dpar_ref)
        dskip_ref[...] = jnp.zeros_like(dskip_ref)

    d_exit = d_state[...]
    for u in reversed(range(PAIR)):
        rows = slice(CHUNK * u, CHUNK * (u + 1))
        b, c, raw, step, logs, step_w, carry_w, tail_w, inner, decays, drive = chunk_values(
            u, x_ref, bcr_ref, flags_ref, seg_col, seg_row, par_ref
        )
        x, z = x_ref[rows, :], z_ref[rows, :]
        g = g_ref[0, u, 0].astype(F32).T
        sig = jax.nn.sigmoid(z)
        dy = g * z * sig
        dz_ref[rows, :] = (g * y_ref[rows, :] * (sig * (1.0 + z * (1.0 - sig)))).astype(BF)
        entry = entry_ref[u]
        c_entry = mm(c, entry)
        carried = carry_w * dy
        tailed = tail_w * drive
        piece = carry_w[CHUNK - 1 : CHUNK, :]
        dys = by_head(dy)
        kernels, cols = [], []
        row_sums = jnp.zeros((CHUNK, 8), F32)
        d_inner = jnp.zeros((CHUNK, CHUNK), F32)
        place = lax.broadcasted_iota(jnp.int32, (CHUNK, 8), 1)
        drive_low = drive.astype(BF)
        for h in range(SLOTS):
            kernel = decays[h] * inner
            d_kernel = mm(dys[h], drive_low, 1, 1)
            d_inner = d_inner + decays[h] * d_kernel
            d_gap = kernel * d_kernel
            row_sums = row_sums + jnp.where(place == h, jnp.sum(d_gap, axis=1, keepdims=True), 0.0)
            cols.append(jnp.sum(d_gap, axis=0, keepdims=True))
            kernels.append(kernel.astype(BF))
        cols = jnp.concatenate(cols + [jnp.zeros((8 - SLOTS, CHUNK), F32)], axis=0).T
        d_drive = mm(jnp.concatenate(kernels, axis=0), jnp.concatenate(dys, axis=0), 0, 0)
        b_exit = mm(b, d_exit)
        d_drive = d_drive + tail_w * b_exit
        dx_ref[rows, :] = (step_w * d_drive + skip_ref[...] * dy).astype(BF)
        dskip_ref[...] += jnp.sum(dy * x, axis=0, keepdims=True)
        ends = jnp.sum(entry * d_exit, axis=0, keepdims=True) * piece
        sums = mm32(
            jnp.concatenate(
                [d_drive * x, carried * c_entry, tailed * b_exit, jnp.broadcast_to(ends, (8, LANES))], axis=0
            ),
            head_selector(True),
        )
        d_step, from_carry, from_tail = sums[:CHUNK], sums[CHUNK : 2 * CHUNK], sums[2 * CHUNK : 3 * CHUNK]
        d_last = jnp.sum(from_tail, axis=0, keepdims=True) + sums[3 * CHUNK : 3 * CHUNK + 1]
        d_cum = row_sums - cols + from_carry - from_tail
        row = lax.broadcasted_iota(jnp.int32, (CHUNK, CHUNK), 0)
        col = lax.broadcasted_iota(jnp.int32, (CHUNK, CHUNK), 1)
        d_logs = mm32((row <= col).astype(F32), d_cum) + d_last
        d_step = d_step + d_logs * par_ref[0:1, :]
        d_raw = d_step * jax.nn.sigmoid(raw)
        dpar_ref[0:1, :] += jnp.sum(d_logs * logs, axis=0, keepdims=True)
        dpar_ref[1:2, :] += jnp.sum(d_raw, axis=0, keepdims=True)
        d_b = mm(d_inner, c, 0, 0) + mm(tailed, d_exit, 1, 1)
        d_c = mm(d_inner, b) + mm(carried, entry, 1, 1)
        dbcr_ref[rows, :] = jnp.concatenate(
            [d_b, d_c, d_raw, jnp.zeros((CHUNK, 128 - 2 * NS - 8), F32)], axis=1
        ).astype(BF)
        d_exit = piece * d_exit + mm(c, carried, 0, 0)
    d_state[...] = d_exit


def owner_block(place):
    return pl.BlockSpec(
        (1, PAIR, 1, LANES, CHUNK), lambda i: (place(i) // 4, 0, place(i) % 4, 0, 0)
    )


def state_specs(place):
    return [
        pl.BlockSpec((STEP, LANES), lambda i: (place(i), 1)),
        pl.BlockSpec((STEP, LANES), lambda i: (place(i), 2)),
        pl.BlockSpec((STEP, 128), lambda i: (place(i), 6)),
        pl.BlockSpec((STEP, 2), lambda i: (place(i), 0)),
        pl.BlockSpec((STEP, 1), lambda i: (place(i), 0)),
        pl.BlockSpec((1, STEP), lambda i: (0, place(i))),
        pl.BlockSpec((2, 8), lambda i: (0, 0)),
        pl.BlockSpec((1, LANES), lambda i: (0, 0)),
    ]


def states(projected, flags, seg_col, seg_row, par, skip):
    return pl.pallas_call(
        state_kernel,
        grid=(STEPS,),
        in_specs=state_specs(lambda i: i),
        out_specs=[
            owner_block(lambda i: i),
            pl.BlockSpec((STEP, LANES), lambda i: (i, 0)),
            pl.BlockSpec((PAIR, NS, LANES), lambda i: (i, 0, 0)),
        ],
        out_shape=[
            jax.ShapeDtypeStruct((2, 2, 4, LANES, CHUNK), BF),
            jax.ShapeDtypeStruct((LENGTH, LANES), F32),
            jax.ShapeDtypeStruct((CHUNKS, NS, LANES), F32),
        ],
        scratch_shapes=[pltpu.VMEM((NS, LANES), F32)],
        compiler_params=pltpu.CompilerParams(vmem_limit_bytes=VMEM_LIMIT),
        cost_estimate=pl.CostEstimate(flops=1_500_000_000, bytes_accessed=10_000_000, transcendentals=2_000_000),
        name="states",
    )(projected, projected, projected, flags, seg_col, seg_row, par, skip)


def states_back(projected, flags, seg_col, seg_row, par, skip, y, entry, g):
    def back(i):
        return STEPS - 1 - i

    return pl.pallas_call(
        state_back_kernel,
        grid=(STEPS,),
        in_specs=state_specs(back)
        + [
            pl.BlockSpec((STEP, LANES), lambda i: (back(i), 0)),
            pl.BlockSpec((PAIR, NS, LANES), lambda i: (back(i), 0, 0)),
            owner_block(back),
        ],
        out_specs=[
            pl.BlockSpec((STEP, LANES), lambda i: (back(i), 0)),
            pl.BlockSpec((STEP, LANES), lambda i: (back(i), 0)),
            pl.BlockSpec((STEP, 128), lambda i: (back(i), 0)),
            pl.BlockSpec((2, 8), lambda i: (0, 0)),
            pl.BlockSpec((1, LANES), lambda i: (0, 0)),
        ],
        out_shape=[
            jax.ShapeDtypeStruct((LENGTH, LANES), BF),
            jax.ShapeDtypeStruct((LENGTH, LANES), BF),
            jax.ShapeDtypeStruct((LENGTH, 128), BF),
            jax.ShapeDtypeStruct((2, 8), F32),
            jax.ShapeDtypeStruct((1, LANES), F32),
        ],
        scratch_shapes=[pltpu.VMEM((NS, LANES), F32)],
        compiler_params=pltpu.CompilerParams(vmem_limit_bytes=VMEM_LIMIT),
        cost_estimate=pl.CostEstimate(flops=4_000_000_000, bytes_accessed=12_000_000, transcendentals=3_000_000),
        name="states_back",
    )(projected, projected, projected, flags, seg_col, seg_row, par, skip, y, entry, g)


def once(*shape):
    return pl.BlockSpec(shape, lambda i: (0,) * len(shape), pipeline_mode=pl.Buffered(1))


def place_kernel(where_ref, *refs):
    *blocks, out_ref = refs
    for h in range(2):
        near, right, far_top, far_low, left = blocks[5 * h : 5 * h + 5]
        half = lax.rem(where_ref[0] + h, 2) * 4
        spots = [half + lax.rem(where_ref[1] + k, 4) for k in range(4)]
        out_ref[spots[0]] = near[...]
        out_ref[spots[1]] = right[...]
        out_ref[spots[2], :64] = far_top[...]
        out_ref[spots[2], 64:] = far_low[...]
        out_ref[spots[3]] = left[...]


def place(where, blocks):
    return pl.pallas_call(
        place_kernel,
        grid=(1,),
        in_specs=[pl.BlockSpec(memory_space=pltpu.SMEM)] + [once(*v.shape) for v in blocks],
        out_specs=once(8, ROWS + 16, WIDTH),
        out_shape=jax.ShapeDtypeStruct((8, ROWS + 16, WIDTH), BF),
        compiler_params=pltpu.CompilerParams(vmem_limit_bytes=VMEM_LIMIT),
        cost_estimate=pl.CostEstimate(flops=0, bytes_accessed=9_000_000, transcendentals=0),
        name="place",
    )(where, *blocks)


def spread_kernel(attention_ref, mixer_ref, param_ref, out_ref):
    attention, mixer, param = attention_ref[...], mixer_ref[...], param_ref[...]

    def empty(width):
        return jnp.zeros((100, width), BF)

    for s in range(PEERS):
        group, pair = s // 3, s % 3
        if s == 15:
            parts = [empty(256)]
        else:
            at = 64 * (5 * group + 2 * pair)
            width = 128 if pair < 2 else 64
            parts = [attention[:, at : at + width]] + [empty(128 - width)] * (pair == 2)
            parts += [attention[:, at : at + 64] for at in (1600 + 64 * group, 1920 + 64 * group)]
        for side in (0, DI):
            parts.append(mixer[:, side + 192 * s : side + 192 * (s + 1)])
            at = side + 48 * 64 + 64 * s
            parts.append(mixer[:, at : at + 64] if s < 2 else empty(64))
        parts += [param[:, : 2 * NS], param[:, 2 * NS + 3 * s : 2 * NS + 3 * (s + 1)]]
        parts.append(param[:, 80 + s : 81 + s] if s < 2 else empty(1))
        parts.append(empty(128 - 2 * NS - SLOTS))
        out_ref[s] = jnp.concatenate(parts, axis=1)


def spread_inputs(attention, mixer, param):
    return pl.pallas_call(
        spread_kernel,
        grid=(1,),
        in_specs=[once(*v.shape) for v in (attention, mixer, param)],
        out_specs=once(PEERS, 100, IN_WIDTH),
        out_shape=jax.ShapeDtypeStruct((PEERS, 100, IN_WIDTH), BF),
        compiler_params=pltpu.CompilerParams(vmem_limit_bytes=VMEM_LIMIT),
        cost_estimate=pl.CostEstimate(flops=0, bytes_accessed=5_000_000, transcendentals=0),
        name="spread",
    )(attention, mixer, param)


def in_order(core, mine, other):
    first = jnp.where(core == 0, mine, other)
    second = jnp.where(core == 0, other, mine)
    return first, second


def project_kernel(core_ref, mine_ref, other_ref, gain_ref, weight_ref, normed_ref, out_ref, kv_ref, kvt_ref):
    mine, other = mine_ref[0, :ROWS, :].astype(F32), other_ref[0, :ROWS, :].astype(F32)
    tok = jnp.concatenate(in_order(core_ref[0], mine, other), axis=0)
    scale = lax.rsqrt(jnp.mean(tok * tok, axis=-1, keepdims=True) + 1e-06)
    normed = (tok * scale * gain_ref[...]).astype(BF)
    normed_ref[...] = normed
    projected = mm(normed, weight_ref[...])
    out_ref[...] = projected
    kv = projected[:, 128:256]
    kv_ref[...] = kv.astype(BF)
    kvt_ref[...] = kv.T.astype(BF)


def project(core, mine, other, gain, weight):
    return pl.pallas_call(
        project_kernel,
        grid=(8,),
        in_specs=[
            pl.BlockSpec(memory_space=pltpu.SMEM),
            pl.BlockSpec((1, ROWS + 16, WIDTH), lambda i: (i, 0, 0)),
            pl.BlockSpec((1, ROWS + 16, WIDTH), lambda i: (i, 0, 0)),
            once(1, WIDTH),
            once(WIDTH, IN_WIDTH),
        ],
        out_specs=[
            pl.BlockSpec((2 * ROWS, WIDTH), lambda i: (i, 0)),
            pl.BlockSpec((2 * ROWS, IN_WIDTH), lambda i: (i, 0)),
            pl.BlockSpec((2 * ROWS, 128), lambda i: (i, 0)),
            pl.BlockSpec((128, 2 * ROWS), lambda i: (0, i)),
        ],
        out_shape=[
            jax.ShapeDtypeStruct((LENGTH, WIDTH), BF),
            jax.ShapeDtypeStruct((LENGTH, IN_WIDTH), F32),
            jax.ShapeDtypeStruct((LENGTH, 128), BF),
            jax.ShapeDtypeStruct((128, LENGTH), BF),
        ],
        compiler_params=pltpu.CompilerParams(vmem_limit_bytes=VMEM_LIMIT),
        cost_estimate=pl.CostEstimate(
            flops=8_000_000_000, bytes_accessed=24_000_000, transcendentals=0
        ),
        name="project",
    )(core, mine, other, gain, weight)


def store_parts(refs, values):
    for ref, (start, stop) in zip(refs, ((0, 128), (128, 256), (256, 320), (320, 384), (384, 512))):
        ref[...] = values[start:stop].astype(BF)


def feed_kernel(*refs):
    feeds, grads, gate_ups, downs = refs[:5], refs[5:10], refs[10:14], refs[14:18]
    feed_ref, grad_ref, hidden_ref, d_gate_up_ref = refs[18:22]
    for parts, target in ((feeds, feed_ref), (grads, grad_ref)):
        at = 0
        for part in parts:
            target[at : at + part.shape[0], :] = part[...]
            at += part.shape[0]
    feed, grad = feed_ref[...], grad_ref[...]
    out = jnp.zeros((512, WIDTH), F32)
    d_feed = jnp.zeros((512, WIDTH), F32)
    for b in range(4):
        gate_up = mm(feed, gate_ups[b][...], 1, 1)
        d_hidden = mm(grad, downs[b][...], 1, 1)
        gate, up = gate_up[:, :FF_ROWS], gate_up[:, FF_ROWS:]
        sigmoid = jax.nn.sigmoid(gate)
        silu = gate * sigmoid
        hidden = (silu * up).astype(BF)
        d_gate = d_hidden * up * (sigmoid * (1.0 + gate * (1.0 - sigmoid)))
        d_gate_up = jnp.concatenate([d_gate, d_hidden * silu], axis=1).astype(BF)
        hidden_ref[b] = hidden
        d_gate_up_ref[b] = d_gate_up
        out = out + mm(hidden, downs[b][...])
        d_feed = d_feed + mm(d_gate_up, gate_ups[b][...])
    store_parts(refs[22:27], out)
    store_parts(refs[27:32], d_feed)


def feed_forward(feeds, grads, gate_ups, downs):
    parts = [(ROWS, WIDTH), (ROWS, WIDTH), (64, WIDTH), (64, WIDTH), (ROWS, WIDTH)]
    shapes = [(512, WIDTH)] * 2 + [(4, 512, FF_ROWS), (4, 512, 2 * FF_ROWS)] + parts + parts
    return pl.pallas_call(
        feed_kernel,
        grid=(1,),
        in_specs=[once(*v.shape) for v in (*feeds, *grads, *gate_ups, *downs)],
        out_specs=[once(*shape) for shape in shapes],
        out_shape=[jax.ShapeDtypeStruct(shape, BF) for shape in shapes],
        compiler_params=pltpu.CompilerParams(vmem_limit_bytes=VMEM_LIMIT),
        cost_estimate=pl.CostEstimate(
            flops=25_000_000_000, bytes_accessed=28_000_000, transcendentals=700_000
        ),
        name="feed_forward",
    )(*feeds, *grads, *gate_ups, *downs)


def feed_grads_kernel(feed_ref, grad_ref, hidden_ref, d_gate_up_ref, near_ref, far_ref):
    for b, out_ref in enumerate((near_ref, far_ref)):
        gate_up = mm(d_gate_up_ref[b], feed_ref[...], 0, 0)
        down = mm(hidden_ref[b], grad_ref[...], 0, 0)
        empty = jnp.zeros((8 * FF_BLOCK - 3 * FF_ROWS, WIDTH), F32)
        together = jnp.concatenate([gate_up, down, empty], axis=0).astype(BF)
        for i in range(8):
            out_ref[i] = together[FF_BLOCK * i : FF_BLOCK * (i + 1)]


def feed_grads(half, feed, grad, hidden, d_gate_up):
    return pl.pallas_call(
        feed_grads_kernel,
        grid=(1,),
        in_specs=[
            once(512, WIDTH),
            once(512, WIDTH),
            pl.BlockSpec((2, 512, FF_ROWS), lambda i: (half, 0, 0), pipeline_mode=pl.Buffered(1)),
            pl.BlockSpec((2, 512, 2 * FF_ROWS), lambda i: (half, 0, 0), pipeline_mode=pl.Buffered(1)),
        ],
        out_specs=[once(8, FF_BLOCK, WIDTH)] * 2,
        out_shape=[jax.ShapeDtypeStruct((8, FF_BLOCK, WIDTH), BF)] * 2,
        compiler_params=pltpu.CompilerParams(vmem_limit_bytes=VMEM_LIMIT),
        cost_estimate=pl.CostEstimate(
            flops=5_000_000_000, bytes_accessed=12_000_000, transcendentals=0
        ),
        name="feed_grads",
    )(feed, grad, hidden, d_gate_up)


def in_grads_kernel(normed_ref, *refs):
    *parts, weight_ref, small_ref, out_ref, acc = refs
    step = pl.program_id(0)

    @pl.when(step == 0)
    def _():
        acc[...] = jnp.zeros_like(acc)

    acc[...] += mm(normed_ref[...], jnp.concatenate([part[...] for part in parts], axis=1), 0, 0)

    @pl.when(step == 7)
    def _():
        width = acc.shape[1]
        product = acc[...] * weight_ref[...].astype(F32)
        gain = mm32(jnp.ones((8, width), F32), product, 1, 1)[:1]
        for s in range(PEERS):
            own_gain = jnp.pad(gain[:, 100 * s : 100 * (s + 1)], ((0, 0), (width - 128, 28)))
            out_ref[s] = jnp.concatenate(
                [acc[100 * s : 100 * (s + 1), :], small_ref[s : s + 1, :] + own_gain, jnp.zeros((3, width), F32)],
                axis=0,
            ).astype(BF)


def projected_specs():
    return [
        pl.BlockSpec((256, 128), lambda i: (i, 0)),
        pl.BlockSpec((256, 128), lambda i: (i, 0)),
        pl.BlockSpec((256, 256), lambda i: (i, 0)),
        pl.BlockSpec((256, 256), lambda i: (i, 0)),
        pl.BlockSpec((256, 128), lambda i: (i, 0)),
    ]


def in_grads(normed, parts, weight, small):
    width = weight.shape[1]
    return pl.pallas_call(
        in_grads_kernel,
        grid=(8,),
        in_specs=[pl.BlockSpec((256, WIDTH), lambda i: (i, 0))]
        + [pl.BlockSpec((256, part.shape[1]), lambda i: (i, 0)) for part in parts]
        + [once(WIDTH, width), once(PEERS, width)],
        out_specs=once(PEERS, 104, width),
        out_shape=jax.ShapeDtypeStruct((PEERS, 104, width), BF),
        scratch_shapes=[pltpu.VMEM((WIDTH, width), F32)],
        compiler_params=pltpu.CompilerParams(vmem_limit_bytes=VMEM_LIMIT),
        cost_estimate=pl.CostEstimate(
            flops=10 * LENGTH * width * 1000, bytes_accessed=14_000_000, transcendentals=0
        ),
        name="in_grads",
    )(normed, *parts, weight, small)


def d_normed_kernel(core_ref, q_ref, kv_ref, x_ref, z_ref, bcr_ref, weight_ref, kept_ref, sent_ref):
    parts = [q_ref[...], kv_ref[...], x_ref[...], z_ref[...], bcr_ref[...]]
    d_normed = mm(jnp.concatenate(parts, axis=1), weight_ref[...], 1, 1)
    kept, sent = in_order(core_ref[0], d_normed[:ROWS], d_normed[ROWS:])
    kept_ref[0] = kept.astype(BF)
    sent_ref[0] = sent.astype(BF)


def d_normed_parts(core, d_parts, weight):
    return pl.pallas_call(
        d_normed_kernel,
        grid=(8,),
        in_specs=[pl.BlockSpec(memory_space=pltpu.SMEM)] + projected_specs() + [once(WIDTH, IN_WIDTH)],
        out_specs=[pl.BlockSpec((1, ROWS, WIDTH), lambda i: (i, 0, 0))] * 2,
        out_shape=[jax.ShapeDtypeStruct((8, ROWS, WIDTH), BF)] * 2,
        compiler_params=pltpu.CompilerParams(vmem_limit_bytes=VMEM_LIMIT),
        cost_estimate=pl.CostEstimate(
            flops=8_000_000_000, bytes_accessed=13_000_000, transcendentals=0
        ),
        name="d_normed",
    )(core, *d_parts, weight)


def rep_spots(z_ref, pieces):
    near, right, far_top, far_low, left = pieces
    spots = [2 * lax.rem(z_ref[0] + k, 4) for k in range(4)]
    pairs = [(spots[0], near), (spots[1], right), (spots[3], left)]
    single = [(spots[2], far_top[...]), (spots[2] + 1, far_low[...])]
    return single + [(spot + yl, pair[yl]) for spot, pair in pairs for yl in range(2)]


def collect_kernel(z_ref, *refs):
    pieces, refs = refs[:5], refs[5:]
    heads_ref, attention_ref, mixer_ref, param_ref, low_states_ref, low_heads_ref, states_ref = refs
    for spot, block in rep_spots(z_ref, pieces):
        for i in range(2):
            states_ref[2 * spot + i] = block[i]
    shared = jnp.zeros((104, 128), F32)
    low_states_ref[...] = jnp.zeros_like(low_states_ref)
    low_heads_ref[...] = jnp.zeros_like(low_heads_ref)
    for s in range(PEERS):
        tile = heads_ref[s].astype(F32)
        low_heads_ref[s : s + 1, :] = tile[100:101, :]
        if s < 15:
            width = 128 if s % 3 < 2 else 64
            at = 64 * (5 * (s // 3) + 2 * (s % 3))
            attention_ref[:, at : at + width] = tile[:100, :width]
        tile = states_ref[s].astype(F32)
        low_states_ref[s : s + 1, :] = tile[100:101, :]
        for side in range(2):
            part = tile[:100, 256 * side : 256 * (side + 1)]
            at = DI * side + 192 * s
            mixer_ref[:, at : at + 192] = part[:, :192]
            if s < 2:
                at = DI * side + 48 * 64 + 64 * s
                mixer_ref[:, at : at + 64] = part[:, 192:]
        raw = tile[:, 512:]
        shared = shared + raw
        at = 2 * NS + 3 * s
        param_ref[:, at : at + 3] = raw[:100, 2 * NS : 2 * NS + 3]
        if s < 2:
            param_ref[:, 80 + s : 81 + s] = raw[:100, 2 * NS + 3 : 2 * NS + 4]
    param_ref[:, : 2 * NS] = shared[:100, : 2 * NS]
    for k in range(KV_HEADS):
        kv = sum(heads_ref[3 * k + j].astype(F32)[:100, 128:] for j in range(3))
        attention_ref[:, 1600 + 64 * k : 1664 + 64 * k] = kv[:, :64]
        attention_ref[:, 1920 + 64 * k : 1984 + 64 * k] = kv[:, 64:]


def collect(z, states_pieces, heads_rows):
    return pl.pallas_call(
        collect_kernel,
        grid=(1,),
        in_specs=[pl.BlockSpec(memory_space=pltpu.SMEM)]
        + [once(*v.shape) for v in (*states_pieces, heads_rows)],
        out_specs=[once(100, 2240), once(100, 2 * DI), once(100, 82), once(PEERS, 640), once(PEERS, 256)],
        out_shape=[
            jax.ShapeDtypeStruct((100, 2240), F32),
            jax.ShapeDtypeStruct((100, 2 * DI), F32),
            jax.ShapeDtypeStruct((100, 82), F32),
            jax.ShapeDtypeStruct((PEERS, 640), F32),
            jax.ShapeDtypeStruct((PEERS, 256), F32),
        ],
        scratch_shapes=[pltpu.VMEM((PEERS, 104, 640), BF)],
        compiler_params=pltpu.CompilerParams(vmem_limit_bytes=VMEM_LIMIT),
        cost_estimate=pl.CostEstimate(flops=0, bytes_accessed=7_000_000, transcendentals=0),
        name="collect",
    )(z, *states_pieces, heads_rows)


def line_tokens(act, source, x):
    return jnp.concatenate([act[source, lax.rem(x + k, 4)] for k in range(4)], axis=1)


def out_kernel(where_ref, att_ref, mix_ref, w00, w01, w10, w11, *outs):
    att = jnp.zeros((512, WIDTH), F32)
    mix = jnp.zeros((512, WIDTH), F32)
    for a, b, weight in ((0, 0, w00), (0, 1, w01), (1, 0, w10), (1, 1, w11)):
        source = lax.rem(where_ref[0] + a, 2) * 2 + lax.rem(where_ref[2] + b, 2)
        mix = mix + mm(line_tokens(mix_ref, source, where_ref[1]), weight[:LANES, :], 0, 0)
        att = att + mm(line_tokens(att_ref, source, where_ref[1]), weight[LANES:, :], 0, 0)
    for k, ref in ((0, outs[0]), (1, outs[1]), (3, outs[4])):
        ref[:ROWS, :] = att[ROWS * k : ROWS * (k + 1)].astype(BF)
        ref[ROWS:, :] = mix[ROWS * k : ROWS * (k + 1)].astype(BF)
    outs[2][...] = att[2 * ROWS : 3 * ROWS].astype(BF)
    outs[3][...] = mix[2 * ROWS : 3 * ROWS].astype(BF)


def out_projections(where, att, mix, weights):
    two, one = (2 * ROWS, WIDTH), (ROWS, WIDTH)
    shapes = (two, two, one, one, two)
    return pl.pallas_call(
        out_kernel,
        grid=(1,),
        in_specs=[pl.BlockSpec(memory_space=pltpu.SMEM)] + [once(*v.shape) for v in (att, mix, *weights)],
        out_specs=[once(*shape) for shape in shapes],
        out_shape=[jax.ShapeDtypeStruct(shape, BF) for shape in shapes],
        compiler_params=pltpu.CompilerParams(vmem_limit_bytes=VMEM_LIMIT),
        cost_estimate=pl.CostEstimate(
            flops=5_000_000_000, bytes_accessed=10_000_000, transcendentals=0
        ),
        name="out_projections",
    )(where, att, mix, *weights)


def out_back_kernel(where_ref, near, right, far_top, far_low, left, att_ref, mix_ref, w00, w01, w10, w11, *outs):
    d_att_ref, d_mix_ref, *grads = outs
    d_att = jnp.concatenate([near[:ROWS, :], right[:ROWS, :], far_top[...], left[:ROWS, :]], axis=0)
    d_mix = jnp.concatenate([near[ROWS:, :], right[ROWS:, :], far_low[...], left[ROWS:, :]], axis=0)
    x = where_ref[1]
    for a, b, weight, grad in (
        (0, 0, w00, grads[0]),
        (0, 1, w01, grads[1]),
        (1, 0, w10, grads[2]),
        (1, 1, w11, grads[3]),
    ):
        source = lax.rem(where_ref[0] + a, 2) * 2 + lax.rem(where_ref[2] + b, 2)
        d_mix_part = mm(weight[:LANES, :], d_mix, 1, 1).astype(BF)
        d_att_part = mm(weight[LANES:, :], d_att, 1, 1).astype(BF)
        for k in range(4):
            d_mix_ref[source, lax.rem(x + k, 4)] = d_mix_part[:, ROWS * k : ROWS * (k + 1)]
            d_att_ref[source, lax.rem(x + k, 4)] = d_att_part[:, ROWS * k : ROWS * (k + 1)]
        grad_mix = mm(line_tokens(mix_ref, source, x), d_mix)
        grad_att = mm(line_tokens(att_ref, source, x), d_att)
        together = jnp.concatenate([grad_mix, grad_att], axis=0).astype(BF)
        for i in range(8):
            grad[i] = together[OUT_BLOCK * i : OUT_BLOCK * (i + 1)]


def out_projections_back(where, d_proj, att, mix, weights):
    return pl.pallas_call(
        out_back_kernel,
        grid=(1,),
        in_specs=[pl.BlockSpec(memory_space=pltpu.SMEM)]
        + [once(*v.shape) for v in (*d_proj, att, mix, *weights)],
        out_specs=[once(4, 4, 128, ROWS), once(4, 4, LANES, ROWS)] + [once(8, OUT_BLOCK, WIDTH)] * 4,
        out_shape=[
            jax.ShapeDtypeStruct((4, 4, 128, ROWS), BF),
            jax.ShapeDtypeStruct((4, 4, LANES, ROWS), BF),
        ]
        + [jax.ShapeDtypeStruct((8, OUT_BLOCK, WIDTH), BF)] * 4,
        compiler_params=pltpu.CompilerParams(vmem_limit_bytes=VMEM_LIMIT),
        cost_estimate=pl.CostEstimate(
            flops=10_000_000_000, bytes_accessed=20_000_000, transcendentals=0
        ),
        name="out_projections_back",
    )(where, *d_proj, att, mix, *weights)


def halve_kernel(where_ref, kept_ref, came_ref, p0, p1, p2_top, p2_low, p3):
    for k, targets in ((0, (p0, p0)), (1, (p1, p1)), (2, (p2_top, p2_low)), (3, (p3, p3))):
        for h in range(2):
            spot = 4 * h + lax.rem(where_ref[1] + k, 4)
            total = (kept_ref[spot].astype(F32) + came_ref[spot].astype(F32)).astype(BF)
            if k == 2:
                targets[h][...] = total
            else:
                targets[h][ROWS * h : ROWS * (h + 1), :] = total


def halve(where, kept, came):
    two, one = (2 * ROWS, WIDTH), (ROWS, WIDTH)
    shapes = (two, two, one, one, two)
    return pl.pallas_call(
        halve_kernel,
        grid=(1,),
        in_specs=[pl.BlockSpec(memory_space=pltpu.SMEM), once(8, ROWS, WIDTH), once(8, ROWS, WIDTH)],
        out_specs=[once(*shape) for shape in shapes],
        out_shape=[jax.ShapeDtypeStruct(shape, BF) for shape in shapes],
        compiler_params=pltpu.CompilerParams(vmem_limit_bytes=VMEM_LIMIT),
        cost_estimate=pl.CostEstimate(flops=3_000_000, bytes_accessed=10_000_000, transcendentals=0),
        name="halve",
    )(where, kept, came)


def y_parts_kernel(yl_ref, near_0, came_0, near_1, came_1, p0, p1, p2_top, p2_low, p3):
    def total(half, at, count):
        near, came = ((near_0, came_0), (near_1, came_1))[half]
        rows = slice(at, at + count)
        return (near[rows].astype(F32) + came[rows].astype(F32)).astype(BF)

    for yl in range(2):

        @pl.when(yl_ref[0] == yl)
        def _():
            p0[...] = total(0, 4 * yl, 4)
            p1[...] = total(yl, 4 * (1 - yl), 4)
            p2_top[...] = total(1, 4 * yl, 2)
            p2_low[...] = total(1, 4 * yl + 2, 2)
            p3[...] = total(1 - yl, 4 * (1 - yl), 4)


def y_parts(yl, near_0, came_0, near_1, came_1):
    block = near_0.shape[1:]
    shapes = [(count,) + block for count in (4, 4, 2, 2, 4)]
    return pl.pallas_call(
        y_parts_kernel,
        grid=(1,),
        in_specs=[pl.BlockSpec(memory_space=pltpu.SMEM)] + [once(*near_0.shape)] * 4,
        out_specs=[once(*shape) for shape in shapes],
        out_shape=[jax.ShapeDtypeStruct(shape, BF) for shape in shapes],
        compiler_params=pltpu.CompilerParams(vmem_limit_bytes=VMEM_LIMIT),
        cost_estimate=pl.CostEstimate(flops=4_000_000, bytes_accessed=20_000_000, transcendentals=0),
        name="y_parts",
    )(yl, near_0, came_0, near_1, came_1)


def z_parts_kernel(z_ref, *refs):
    ff, out, parts = refs[:3], refs[3:7], refs[7:]

    def total(terms, k):
        at = lax.rem(z_ref[0] + k, 4)
        return sum(term[at].astype(F32) for term in terms)

    for k in range(4):
        empty = jnp.zeros((RING_ROWS - FF_BLOCK - OUT_BLOCK, WIDTH), F32)
        block = jnp.concatenate([total(out, k), total(ff, k), empty], axis=0).astype(BF)
        if k == 2:
            parts[2][...] = block[: RING_ROWS // 2]
            parts[3][...] = block[RING_ROWS // 2 :]
        else:
            parts[(0, 1, 2, 4)[k]][...] = block


def z_parts(z, ff, out):
    one, half = (RING_ROWS, WIDTH), (RING_ROWS // 2, WIDTH)
    shapes = (one, one, half, half, one)
    return pl.pallas_call(
        z_parts_kernel,
        grid=(1,),
        in_specs=[pl.BlockSpec(memory_space=pltpu.SMEM)] + [once(*v.shape) for v in (*ff, *out)],
        out_specs=[once(*shape) for shape in shapes],
        out_shape=[jax.ShapeDtypeStruct(shape, BF) for shape in shapes],
        compiler_params=pltpu.CompilerParams(vmem_limit_bytes=VMEM_LIMIT),
        cost_estimate=pl.CostEstimate(flops=4_000_000, bytes_accessed=10_000_000, transcendentals=0),
        name="z_parts",
    )(z, *ff, *out)


def one_hot(rows, columns, offset, limit=None):
    row = lax.broadcasted_iota(jnp.int32, (rows, columns), 0)
    column = lax.broadcasted_iota(jnp.int32, (rows, columns), 1)
    hit = column == row + offset
    if limit is not None:
        hit = hit & (row < limit)
    return hit.astype(F32).astype(BF)


def head_places(me):
    filled = jnp.where(me == 15, 0, jnp.where(lax.rem(me, 3) == 2, HEAD, 2 * HEAD))
    return 20 * lax.div(me, 3) + 28 * lax.rem(me, 3), filled, 200 - 8 * me


def to_heads_kernel(me_ref, att_0, att_1, att_2, mix_before, mix_own, extra_0, extra_1, out_ref):
    att_at, filled, mix_at = head_places(me_ref[0])
    mix = mm(one_hot(192, 200, mix_at), mix_before[...]) + mm(one_hot(192, 200, mix_at - 200), mix_own[...])
    att = jnp.zeros((128, WIDTH), F32)
    for t, rows in enumerate((att_0, att_1, att_2)):
        att = att + mm(one_hot(128, 100, att_at - 100 * t, filled), rows[...])
    out_ref[:192, :] = mix.astype(BF)
    out_ref[192:256, :] = extra_0[...] + extra_1[...]
    out_ref[256:, :] = att.astype(BF)


def to_heads(me, rows):
    return pl.pallas_call(
        to_heads_kernel,
        grid=(1,),
        in_specs=[pl.BlockSpec(memory_space=pltpu.SMEM)] + [once(*v.shape) for v in rows],
        out_specs=once(384, WIDTH),
        out_shape=jax.ShapeDtypeStruct((384, WIDTH), BF),
        compiler_params=pltpu.CompilerParams(vmem_limit_bytes=VMEM_LIMIT),
        cost_estimate=pl.CostEstimate(flops=600_000_000, bytes_accessed=4_000_000, transcendentals=0),
        name="to_heads",
    )(me, *rows)


def finish_kernel(me_ref, z_ref, *refs):
    pieces, refs = refs[:5], refs[5:]
    gateup_ref, down_ref, att_0, att_1, att_2, mix_before, mix_own, extra_ref, blocks_ref, out_ref = refs
    for spot, block in rep_spots(z_ref, pieces):
        blocks_ref[spot] = block
    for half in range(2):
        for z in range(4):
            block = blocks_ref[2 * z + half].astype(F32)
            i = 4 * half + z
            out_ref[OUT_BLOCK * i : OUT_BLOCK * (i + 1), :] = block[:OUT_BLOCK].astype(BF)
            start, stop = FF_BLOCK * i, min(FF_BLOCK * (i + 1), 3 * FF_ROWS)
            rows = block[OUT_BLOCK : OUT_BLOCK + FF_BLOCK]
            edge = 2 * FF_ROWS
            if start < edge:
                end = min(stop, edge)
                gateup_ref[start:end, :] = rows[: end - start]
            if stop > edge:
                begin = max(start, edge)
                down_ref[begin - edge : stop - edge, :] = rows[begin - start : stop - start]
    att_at, filled, mix_at = head_places(me_ref[0])
    mix, att = out_ref[:192, :], out_ref[256:, :]
    for t, target in enumerate((att_0, att_1, att_2)):
        kept = mm(one_hot(128, 100, att_at - 100 * t, filled), att, 0, 0)
        target[...] = kept.astype(BF)
    mix_before[...] = mm(one_hot(192, 200, mix_at), mix, 0, 0).astype(BF)
    mix_own[...] = mm(one_hot(192, 200, mix_at - 200), mix, 0, 0).astype(BF)
    extra_ref[...] = out_ref[192:256, :]


def finish(me, z, pieces):
    shapes = (
        [((2 * FF_ROWS, WIDTH), F32), ((FF_ROWS, WIDTH), F32)]
        + [((100, WIDTH), BF)] * 3
        + [((200, WIDTH), BF)] * 2
        + [((64, WIDTH), BF)]
    )
    return pl.pallas_call(
        finish_kernel,
        grid=(1,),
        in_specs=[pl.BlockSpec(memory_space=pltpu.SMEM)] * 2 + [once(*v.shape) for v in pieces],
        out_specs=[once(*shape) for shape, _ in shapes],
        out_shape=[jax.ShapeDtypeStruct(shape, kind) for shape, kind in shapes],
        scratch_shapes=[
            pltpu.VMEM((8, RING_ROWS, WIDTH), BF),
            pltpu.VMEM((8 * OUT_BLOCK, WIDTH), BF),
        ],
        compiler_params=pltpu.CompilerParams(vmem_limit_bytes=VMEM_LIMIT),
        cost_estimate=pl.CostEstimate(flops=600_000_000, bytes_accessed=16_000_000, transcendentals=0),
        name="finish",
    )(me, z, *pieces)


def root_norm(values, gain):
    return values * lax.rsqrt(jnp.mean(values * values, axis=-1, keepdims=True) + 1e-06) * gain


def branch_sum(attend_proj, mixer_proj, attend_gain, mixer_gain):
    return root_norm(attend_proj, attend_gain) + root_norm(mixer_proj, mixer_gain)


Y = ("yl", "yh")
SIZES = {"x": 4, "z": 4, "core": 2, "yh": 2, "yl": 2, SHARD: PEERS, Y: 4}


def shift(v, axis, by):
    n, shape = SIZES[axis], v.shape
    if shape[-2] % 16 == 0:
        v = v.reshape(shape[:-2] + (shape[-2] // 16, 16, shape[-1]))
    order = (0, 2, 1, 3) if axis == Y else range(n)
    pairs = [(order[i], order[(i + by) % n]) for i in range(n)]
    return lax.ppermute(v, axis, pairs).reshape(shape)


def swap_near(v):
    order, near = (0, 2, 1, 3), (3, 2, 1, 0)
    return lax.ppermute(v, Y, [(order[i], order[near[i]]) for i in range(4)])


def gather_x(v, cut=64):
    left = shift(v, "x", 1)
    right = shift(v, "x", -1)
    return [v, right, shift(left[:cut], "x", 1), shift(right[cut:], "x", -1), left]


def add_low(a, b):
    return (a.astype(F32) + b.astype(F32)).astype(BF)


def ring_first(parts, axis):
    p0, p1, top, low, p3 = parts
    cut = top.shape[0]
    top = shift(top, axis, 1)
    low = shift(low, axis, -1)
    ahead = jnp.concatenate([add_low(p1[:cut], top), p1[cut:]], axis=0)
    behind = jnp.concatenate([p3[:cut], add_low(p3[cut:], low)], axis=0)
    return p0, ahead, behind


def ring_second(p0, ahead, behind, axis):
    return p0, shift(ahead, axis, 1), shift(behind, axis, -1)


def total(terms):
    return sum(term.astype(F32) for term in terms)


def reduce_x(parts):
    return total(ring_second(*ring_first(parts, "x"), "x"))


def spread_sum(blocks, axes):
    came = lax.all_to_all(blocks, axes, 0, 0, tiled=False)
    return jnp.sum(came.astype(F32), axis=0).astype(BF)


def rep_gather(v):
    return lax.all_to_all(jnp.broadcast_to(v[None], (8,) + v.shape), REP, 0, 0, tiled=False)


def collect_states(w):
    n = w.shape[0]
    return jnp.concatenate([w[:, :, :3].reshape(n, 48), w[:, :2, 3]], axis=1)


def local(
    tokens,
    segments,
    input_gain,
    attention_weight,
    attend_out,
    mixer_weight,
    param_weight,
    mixer_out,
    attend_gain,
    mixer_gain,
    feed_gain,
    gateup_weight,
    down_weight,
    decay_log,
    step_bias,
    skip_gain,
    cotangent,
):
    me = lax.axis_index(SHARD)
    yh, x, core = lax.axis_index("yh"), lax.axis_index("x"), lax.axis_index("core")
    where = jnp.stack([yh, x, core]).astype(jnp.int32)
    core_word = where[2:]
    me_word = me.astype(jnp.int32)[None]
    yl_word, z_word = (lax.axis_index(name).astype(jnp.int32)[None] for name in ("yl", "z"))
    grouped = (ROWS // 16, 16, WIDTH)
    tok_low, grad_out = tokens.reshape(grouped), cotangent.reshape(grouped)
    tok = tok_low.astype(F32)
    tok_low, grad_out = tok_low.reshape(ROWS, WIDTH), grad_out.reshape(ROWS, WIDTH)

    gains = jnp.concatenate([input_gain, attend_gain, mixer_gain, feed_gain])
    extra = jnp.concatenate(
        [
            jnp.pad(segments.astype(BF), ((0, 0), (0, WIDTH - ROWS))),
            jnp.pad(gains[None], ((0, 0), (0, WIDTH - 400))),
            jnp.zeros((14, WIDTH), BF),
        ],
        axis=0,
    )
    block = jnp.concatenate([tok_low, extra], axis=0)
    far_block = shift(block, "yh", 1)
    left, right = shift(block, "x", 1), shift(block, "x", -1)
    far_block, left, right, attention_weight, mixer_weight, param_weight = lax.optimization_barrier(
        (far_block, left, right, attention_weight, mixer_weight, param_weight)
    )
    far_left, far_right = shift(far_block, "x", 1), shift(far_block, "x", -1)
    blocks = [block, right, shift(left[:64], "x", 1), shift(right[64:], "x", -1), left]
    spread = spread_inputs(attention_weight, mixer_weight, param_weight).reshape(2, 8, 100, IN_WIDTH)
    spread_other = swap_near(lax.dynamic_index_in_dim(spread, 1 - yh, 0, keepdims=False))
    rows_own = lax.dynamic_index_in_dim(spread, yh, 0, keepdims=False)
    rows_own = lax.all_to_all(rows_own, ("x", "core"), 0, 0, tiled=False)
    rows_own, spread_other, far_left, far_right, blocks = lax.optimization_barrier(
        (rows_own, spread_other, far_left, far_right, blocks)
    )
    blocks += [far_block, far_right, shift(far_left[:64], "x", 1), shift(far_right[64:], "x", -1), far_left]
    rows_other = lax.all_to_all(spread_other, ("x", "core"), 0, 0, tiled=False)
    weight_in = jnp.stack(in_order(yh, rows_own, rows_other)).reshape(WIDTH, IN_WIDTH)
    mine = place(where, blocks)
    other = shift(mine, "core", 1)
    low_rows = jnp.stack(in_order(core, mine[:, ROWS : ROWS + 2, :400], other[:, ROWS : ROWS + 2, :400]), axis=1)
    seg = low_rows[:, :, 0, :ROWS].reshape(LENGTH).astype(jnp.int32)
    all_gains = low_rows[:, :, 1].reshape(PEERS, 4, 100).transpose(1, 0, 2)
    gain_in, gain_attend, gain_mixer, gain_feed = all_gains.reshape(4, WIDTH).astype(F32)

    own_attout, own_mixout, _ = lax.optimization_barrier((attend_out, mixer_out, mine))
    own_heads = to_heads(
        me_word,
        (
            own_attout,
            shift(own_attout, SHARD, -1),
            shift(own_attout, SHARD, -2),
            shift(own_mixout, SHARD, 1),
            own_mixout,
            lax.ppermute(own_mixout[72:136], SHARD, [(15, 0)]),
            lax.ppermute(own_mixout[136:200], SHARD, [(15, 1)]),
        ),
    )
    own_heads, weight_in = lax.optimization_barrier((own_heads, weight_in))
    far_heads = shift(own_heads, "yh", 1)
    own_gateup, _ = lax.optimization_barrier(
        (gateup_weight.transpose(1, 2, 0).reshape(2 * FF_ROWS, WIDTH), spread_other)
    )
    far_gateup = shift(own_gateup, "yh", 1)
    own_down, _ = lax.optimization_barrier((down_weight, own_heads))
    far_down = shift(own_down, "yh", 1)
    normed, projected, kv, kvt = project(core_word, mine, other, gain_in[None], weight_in)
    kv, far_gateup = lax.optimization_barrier((kv, far_gateup))
    seg_col, seg_row = seg[:, None], seg[None]
    attended, logs = attend(projected, kv, kvt, seg_col, seg_row)
    attended = lax.all_to_all(attended.reshape(4, 4, 128, ROWS), ("yh", "core"), 0, 0, tiled=False)
    late_grad_out, far_heads, logs, states_projected = lax.optimization_barrier(
        (grad_out, far_heads, logs, projected)
    )
    some_grad_out = gather_x(late_grad_out)

    slot_heads = jnp.concatenate([3 * me + jnp.arange(3), jnp.minimum(48 + me, 49)[None]])
    valid = jnp.concatenate([jnp.ones((3,), F32), (me < 2).astype(F32)[None]])
    chunk_segs = seg.reshape(LENGTH // CHUNK, CHUNK)
    last = chunk_segs[:, -1]
    before = jnp.concatenate([last[:1] * 0 - 1, last[:-1]])
    flags = jnp.stack(
        [(chunk_segs == before[:, None]).reshape(-1), (chunk_segs == last[:, None]).reshape(-1)], axis=1
    ).astype(F32)
    par = jnp.pad(jnp.stack([-jnp.exp(decay_log[slot_heads]), step_bias[slot_heads]]), ((0, 0), (0, 4)))
    skip = jnp.repeat(skip_gain[slot_heads], 64)[None]
    state_args = (states_projected, flags, seg_col, seg_row, par, skip)
    mixed, states_y, entries = states(*state_args)
    mixed, attended = lax.optimization_barrier((mixed, attended))
    mixed = lax.all_to_all(mixed.reshape(4, 4, LANES, ROWS), ("yh", "core"), 0, 0, tiled=False)

    mixed, far_down = lax.optimization_barrier((mixed, far_down))
    out_weights = [own_heads, shift(own_heads, "core", 1), far_heads, shift(far_heads, "core", 1)]
    downs = [own_down, shift(own_down, "core", 1), far_down, shift(far_down, "core", 1)]
    gateups = [own_gateup, shift(own_gateup, "core", 1), far_gateup, shift(far_gateup, "core", 1)]
    both = reduce_x(out_projections(where, attended, mixed, out_weights)).reshape(2, *grouped)
    attend_proj, mixer_proj = both[0], both[1]
    middle = tok + branch_sum(attend_proj, mixer_proj, gain_attend, gain_mixer)
    feed_in = root_norm(middle, gain_feed).astype(BF).reshape(ROWS, WIDTH)

    fed = feed_forward(gather_x(feed_in), some_grad_out, gateups, downs)
    some_feed, some_grad, hidden, d_gate_up = fed[:4]
    out_parts, d_feed_parts = fed[4:9], fed[9:]
    p0, ahead, behind = ring_first(d_feed_parts, "x")
    near_1, far_1 = feed_grads(1, some_feed, some_grad, hidden, d_gate_up)
    ahead, behind, far_1 = lax.optimization_barrier((ahead, behind, far_1))
    d_feed_in = total(ring_second(p0, ahead, behind, "x")).reshape(grouped)
    far_1 = shift(far_1, "core", 1)

    _, feed_pull = jax.vjp(root_norm, middle, gain_feed)
    middle_part, g_feed = feed_pull(d_feed_in)
    d_middle = grad_out.reshape(grouped).astype(F32) + middle_part
    _, branch_pull = jax.vjp(branch_sum, attend_proj, mixer_proj, gain_attend, gain_mixer)
    d_attproj, d_mixproj, g_attend, g_mixer = branch_pull(d_middle)
    d_both = jnp.stack([d_attproj, d_mixproj]).astype(BF).reshape(2 * ROWS, WIDTH)
    left, right = shift(d_both, "x", 1), shift(d_both, "x", -1)
    near_0, far_0 = feed_grads(0, some_feed, some_grad, hidden, d_gate_up)
    left, right, far_0 = lax.optimization_barrier((left, right, far_0))
    d_proj = [d_both, right, shift(left[:ROWS], "x", 1), shift(right[ROWS:], "x", -1), left]
    far_0 = shift(far_0, "core", 1)
    ff_parts = y_parts(yl_word, near_0, far_0, near_1, far_1)
    out_first_x = ring_first(out_parts, "x")
    d_proj, ff_parts, out_first_x = lax.optimization_barrier((d_proj, ff_parts, out_first_x))
    ff_first = ring_first(ff_parts, Y)
    d_attended, d_mixed, out_00, out_01, out_10, out_11 = out_projections_back(
        where, d_proj, attended, mixed, out_weights
    )
    d_mixed = lax.all_to_all(d_mixed, ("yh", "core"), 0, 0, tiled=False).reshape(2, 2, 4, LANES, ROWS)
    d_attended = lax.all_to_all(d_attended, ("yh", "core"), 0, 0, tiled=False).reshape(2, 2, 4, 128, ROWS)

    out_ring = y_parts(yl_word, out_00, shift(out_01, "core", 1), out_10, shift(out_11, "core", 1))

    out_terms_x = ring_second(*out_first_x, "x")
    d_mixed, out_ring, ff_first, out_terms_x = lax.optimization_barrier(
        (d_mixed, out_ring, ff_first, out_terms_x)
    )
    result = (middle + total(out_terms_x).reshape(grouped)).astype(BF)
    ff_terms = ring_second(*ff_first, Y)
    p0, p1, top, low, p3 = out_ring
    out_terms = [p0, shift(p1, Y, 1), jnp.concatenate([shift(top, Y, 2), shift(low, Y, 2)]), shift(p3, Y, -1)]
    d_x, d_z, d_bcr, d_par, d_skip = states_back(*state_args, states_y, entries, d_mixed)
    d_x, ff_terms, out_terms = lax.optimization_barrier((d_x, ff_terms, out_terms))
    first = ring_first(z_parts(z_word, ff_terms, out_terms), "z")
    heads = jnp.stack([d_par[0, :SLOTS], d_par[1, :SLOTS], d_skip.reshape(SLOTS, 64).sum(axis=1)]) * valid
    heads = jnp.broadcast_to(heads.reshape(1, 3 * SLOTS), (PEERS, 3 * SLOTS))
    small = jnp.concatenate(
        [jnp.pad(g.reshape(PEERS, -1), ((0, 0), (0, 128 - g.size // PEERS))) for g in (g_attend, g_mixer, g_feed, heads)]
        + [jnp.zeros((PEERS, 128), F32)],
        axis=1,
    )
    in_states = in_grads(normed, (d_x, d_z, d_bcr), weight_in[:, 256:], small)
    d_attended, in_states, first = lax.optimization_barrier((d_attended, in_states, first))
    terms = ring_second(*first, "z")
    in_states = lax.all_to_all(in_states, SHARD, 0, 0, tiled=False)
    d_q, d_kv = attend_back(projected, d_attended, kv, kvt, seg_col, seg_row, logs)
    d_q, d_kv, in_states, terms = lax.optimization_barrier((d_q, d_kv, in_states, terms))
    in_states = spread_sum(in_states.reshape(8, 2, 104, 640), REP)
    yl = yl_word[0]
    rep_block = total(terms).astype(BF)
    pair = jnp.stack(in_order(yl, rep_block, shift(rep_block, "yl", 1)))
    in_heads = in_grads(normed, (d_q, d_kv), weight_in[:, :256], jnp.zeros((PEERS, 256), F32))
    in_states, in_heads, d_q, pair = lax.optimization_barrier((in_states, in_heads, d_q, pair))
    left, right = shift(pair, "z", 1), shift(pair, "z", -1)
    in_heads = lax.all_to_all(in_heads, SHARD, 0, 0, tiled=False)
    states_pair = jnp.stack(in_order(yl, in_states, shift(in_states, "yl", 1)))

    kept, sent = d_normed_parts(core_word, (d_q, d_kv, d_x, d_z, d_bcr), weight_in)
    line_parts = halve(where, kept, shift(sent, "core", 1))
    in_heads, line_parts, left, right, states_pair = lax.optimization_barrier(
        (in_heads, line_parts, left, right, states_pair)
    )
    pieces = [pair, right, shift(left[0], "z", 1), shift(right[1], "z", -1), left]
    in_heads = spread_sum(in_heads.reshape(8, 2, 104, 256), REP)
    line_first = ring_first(line_parts, "x")
    states_left, states_right = shift(states_pair, "z", 1), shift(states_pair, "z", -1)
    in_heads, line_first, states_left, states_right = lax.optimization_barrier(
        (in_heads, line_first, states_left, states_right)
    )
    in_heads = rep_gather(in_heads).reshape(PEERS, 104, 256)
    line_terms = ring_second(*line_first, "x")
    states_pieces = [
        states_pair,
        states_right,
        shift(states_left[0], "z", 1),
        shift(states_right[1], "z", -1),
        states_left,
    ]
    line_terms, pieces = lax.optimization_barrier((line_terms, pieces))
    sum_gateup, sum_down, *out_rows = finish(me_word, z_word, pieces)
    in_heads, line_terms, out_rows, states_pieces = lax.optimization_barrier(
        (in_heads, line_terms, out_rows, states_pieces)
    )
    att_0, att_1, att_2, mix_before, mix_own, extra = out_rows
    line = total(line_terms)
    line_kept, line_sent = in_order(yh, line[:ROWS], line[ROWS:])
    d_normed = (line_kept + shift(line_sent.astype(BF), "yh", 1)).reshape(grouped)
    _, input_pull = jax.vjp(lambda t: root_norm(t, gain_in), tok)
    grad_tokens = (d_middle + input_pull(d_normed)[0]).astype(BF)

    sum_attention, sum_mixer, sum_param, low_states, low_heads = collect(z_word, states_pieces, in_heads)
    totals = jnp.sum(low_states, axis=0)
    own_in = (totals[512:612] + jnp.sum(low_heads, axis=0)[128:228]) / input_gain.astype(F32)
    g_decay, g_bias, g_skip = collect_states(
        low_states[:, 384 : 384 + 3 * SLOTS].reshape(PEERS, 3, SLOTS).transpose(1, 0, 2)
    )
    sum_gateup = sum_gateup.reshape(2, FF_ROWS, WIDTH).transpose(2, 0, 1)
    sum_attout = total([att_0, shift(att_1, SHARD, 1), shift(att_2, SHARD, 2)])
    extra_0 = jnp.pad(lax.ppermute(extra, SHARD, [(0, 15)]), ((72, 64), (0, 0)))
    extra_1 = jnp.pad(lax.ppermute(extra, SHARD, [(1, 15)]), ((136, 0), (0, 0)))
    sum_mixout = total([mix_own, shift(mix_before, SHARD, -1), extra_0, extra_1])
    return (
        result.reshape(1, ROWS, WIDTH),
        grad_tokens.reshape(1, ROWS, WIDTH),
        own_in,
        sum_attention,
        sum_attout,
        sum_mixer,
        sum_param,
        sum_mixout,
        totals[:100],
        totals[128:228],
        totals[256:356],
        sum_gateup,
        sum_down,
        g_decay,
        g_bias,
        g_skip,
    )


def solution(mesh):
    fine = Mesh(mesh.devices.reshape(4, 2, 2, 4, 2), ("z", "yl", "yh", "x", "core"))
    rows = P(REP, SHARD, None)
    matrix = P(SHARD, None)
    vector = P(SHARD)
    return jax.shard_map(
        local,
        mesh=fine,
        in_specs=(
            rows,
            P(REP, SHARD),
            vector,
            matrix,
            matrix,
            matrix,
            matrix,
            matrix,
            vector,
            vector,
            vector,
            P(None, None, SHARD),
            matrix,
            P(),
            P(),
            P(),
            rows,
        ),
        out_specs=(
            rows,
            rows,
            vector,
            matrix,
            matrix,
            matrix,
            matrix,
            matrix,
            vector,
            vector,
            vector,
            P(None, None, SHARD),
            matrix,
            P(),
            P(),
            P(),
        ),
        check_vma=False,
    )
```
